256 devices in a mesh: batch: 8 (over y, core), proto: 32 (over x, z).
Axes of the slice: x: 4, y: 4, z: 8, core: 2. Of those that a mesh axis runs over, the one named last changes fastest.
Arguments:
- student_feats: bfloat16 [16384, 256], P(('batch', 'proto')), may hold values from -0.375 to 0.375
- teacher_feats: bfloat16 [16384, 256], P(('batch', 'proto')), may hold values from -0.375 to 0.375
- student_protos: bfloat16 [256, 65536], P(None, 'proto'), may hold values from -1.5 to 1.5
- teacher_protos: bfloat16 [256, 65536], P(None, 'proto'), may hold values from -1.5 to 1.5
Outputs:
- proto_grad: float32 [256, 65536], P('batch', 'proto')
- feature_grad: float32 [16384, 256], P(('batch', 'proto'))
The draws below stay inside these ranges and needn't reach their ends.
All inputs are finite; a program needn't handle non-finite values.
Results may differ from the reference program's by a relative error of at most 0.0089.
Values may be sent and summed in bfloat16 or wider, within the bound.
A program may use at most 128 MiB of HBM per device.

```python
import math
import jax
import jax.numpy as jnp
from jax import lax

D = 256
PROTOS = 65536
CROP_DEV = 2048
ITERS = 3
CROPS = 16384


def draw_teacher_feats(key, part):
    key = jax.random.fold_in(key, 11)
    noise_key, direction_key, weight_key = jax.random.split(key, 3)
    groups = CROPS // CROP_DEV
    direction = jax.random.normal(direction_key, (groups, D), jnp.float32)
    noise = jax.random.normal(noise_key, (CROPS, D), jnp.float32)
    weights = jax.random.uniform(weight_key, (groups,), jnp.float32, 0.3, 2.5)
    shared = jnp.repeat(direction * weights[:, None], CROP_DEV, axis=0, total_repeat_length=CROPS)
    values = 0.03 * (noise + shared)
    return jnp.clip(values, -0.375, 0.375).astype(jnp.bfloat16)


def draw_student_protos(key, part):
    key = jax.random.fold_in(key, 23)
    position = jnp.arange(PROTOS, dtype=jnp.float32) / PROTOS
    spread = 0.22 + 0.07 * position
    noise = jax.random.normal(key, (D, PROTOS), jnp.float32)
    return jnp.clip(noise * spread[None, :], -1.5, 1.5).astype(jnp.bfloat16)


def levels(rng, extent, cuts, low, high):
    level, own = 1.0, jax.random.fold_in(rng, 6)
    for axis_at, parts in cuts:
        heights = jnp.exp(jax.random.uniform(jax.random.fold_in(own, axis_at), (parts,), jnp.float32, low / len(cuts), high / len(cuts)))
        level = level * jnp.repeat(heights, extent[axis_at] // parts).reshape([-1 if axis == axis_at else 1 for axis in range(len(extent))])
    return level


def centred(rng, dims, scale, limit, cuts=(), kind=jnp.bfloat16):
    values = jax.random.normal(rng, dims, jnp.float32) * scale
    if len(cuts) > 0:
        values = levels(rng, dims, cuts, -0.22, 0.18) * values
    return jnp.clip(values, min=-limit, max=limit).astype(kind)


def setup_inputs(seed: int = 0) -> dict:
    streams_of = jax.random.split(jax.random.key(seed), 5)
    return {
        "student_feats": centred(streams_of[0], (CROPS, D), 0.0625, 0.375, ((0, 256),)),
        "teacher_feats": draw_teacher_feats(jax.random.fold_in(streams_of[4], 71), 0),
        "student_protos": draw_student_protos(jax.random.fold_in(streams_of[4], 71), 0),
        "teacher_protos": centred(streams_of[3], (D, PROTOS), 0.25, 1.5, ((1, 32),)),
    }


student_temp = 0.1
teacher_temp = 0.07

def unit_rows(feats):
    values = feats.astype(jnp.float32)
    norm = jnp.sqrt(lax.optimization_barrier(jnp.sum(values * values, axis=1, keepdims=True)) + 1e-06)
    return (values / norm, norm)

def reference(student_feats, teacher_feats, student_protos, teacher_protos):
    stud_unit, stud_norm = unit_rows(student_feats)
    stud_half = stud_unit.astype(jnp.bfloat16)
    teach_unit, teach_norm = unit_rows(teacher_feats)
    teach_half = teach_unit.astype(jnp.bfloat16)
    width = math.gcd(PROTOS, 4096)
    blocks = PROTOS // width
    indices = jnp.arange(blocks, dtype=jnp.int32)

    def columns(protos, index):
        return lax.dynamic_slice_in_dim(protos, (index * width).astype(jnp.int32), width, 1)

    def teacher_block(index):
        return jnp.exp(jnp.dot(teach_half, columns(teacher_protos, index), preferred_element_type=jnp.float32) / teacher_temp)

    def student_block(index):
        return jnp.dot(stud_half, columns(student_protos, index), preferred_element_type=jnp.float32) / student_temp

    def exp_add(total, index):
        return (total + lax.optimization_barrier(jnp.sum(jnp.exp(student_block(index)), axis=1)), None)
    exp_total, _ = lax.scan(exp_add, jnp.zeros((CROPS,), jnp.float32), indices)
    crop_scale = jnp.ones((CROPS,), jnp.float32)
    scale_blocks = jnp.ones((blocks, width), jnp.float32)
    for step in range(ITERS):

        def proto_part(index, weights=crop_scale):
            return jnp.dot(weights, teacher_block(index), precision=lax.Precision.HIGHEST)
        proto_sum = lax.map(proto_part, indices)
        scale_blocks = 1.0 / proto_sum

        def crop_add(total, index, scales=scale_blocks):
            return (total + jnp.dot(teacher_block(index), scales[index], precision=lax.Precision.HIGHEST), None)
        crop_sum, _ = lax.scan(crop_add, jnp.zeros((CROPS,), jnp.float32), indices)
        crop_scale = 1.0 / crop_sum
    lse = jnp.log(exp_total)

    def grad_block(carry, index):
        logits = student_block(index)
        probs = jnp.exp(logits - lse[:, None])
        targets = teacher_block(index) * crop_scale[:, None] * scale_blocks[index][None, :]
        grad_half = (probs - targets).astype(jnp.bfloat16)
        proto_part = lax.dot_general(stud_half, grad_half, (((0,), (0,)), ((), ())), preferred_element_type=jnp.float32) / student_temp
        unit_part = lax.dot_general(grad_half, columns(student_protos, index), (((1,), (1,)), ((), ())), preferred_element_type=jnp.float32) / student_temp
        return (carry + unit_part, proto_part)
    unit_grad, proto_blocks = lax.scan(grad_block, jnp.zeros((CROPS, D), jnp.float32), indices)
    proto_grad = jnp.transpose(proto_blocks, (1, 0, 2)).reshape(D, PROTOS)
    inner = lax.optimization_barrier(jnp.sum(stud_unit * unit_grad, axis=1, keepdims=True))
    feature_grad = (unit_grad - stud_unit * inner) / stud_norm
    return (proto_grad, feature_grad)
```

```python
import functools

import jax
import jax.numpy as jnp
from jax import lax
from jax.experimental import pallas as pl
from jax.experimental.pallas import tpu as pltpu
from jax.sharding import PartitionSpec as P

ITERS = 3
STUDENT_TEMP = 0.1
TEACHER_TEMP = 0.07
LOG2E = 1.4426950408889634
MESH = pl.DeviceIdType.MESH
F32 = jnp.float32
BF16 = jnp.bfloat16
LANES = 128


def unit_rows(feats):
    values = feats.astype(F32)
    norm = jnp.sqrt(jnp.sum(values * values, axis=1, keepdims=True) + 1e-06)
    return values / norm, norm


def kernel(
    nx, nz, ny,
    sf, tf, sp_hbm, tp_hbm,
    pg_out, fg_out,
    tp, sp, spt, tall, uall, ut, m, e, g,
    colacc, ps, payload, cinv, ccs,
    cb, xb, zb_sum, zb,
    ugb, xr, zs, zr,
    pgf, pgb, cr, ys, yr,
    local_s,
    tx_s, tx_r, tr_s, tr_r, tl_s, tl_r,
    ur_s, ur_r, ul_s, ul_r, ux_s, ux_r,
    cb_s, cb_r, ax_s, ax_r, az_s, az_r,
    fx_s, fx_r, fz_s, fz_r, pc_s, pc_r, py_s, py_r,
):
    rows = sf.shape[0]
    depth, width = tp.shape
    block = nx * rows
    crops = nz * block
    nb = 2 * ny
    dr = depth // nb
    tile = min(256, width)
    groups = crops // LANES
    per = block // LANES
    chunk = min(512, width)

    pid = lax.axis_index("proto")
    bid = lax.axis_index("batch")
    x, z = pid // nz, pid % nz
    y, c = bid // 2, bid % 2
    my = pl.multiple_of(x * rows, rows)

    def to_xz(xx, zz):
        return {"proto": (xx % nx) * nz + zz % nz}

    def to_b(bb):
        return {"batch": bb % nb}

    def remote(src, dst, ss, rs, dev):
        return pltpu.make_async_remote_copy(
            src_ref=src, dst_ref=dst, send_sem=ss, recv_sem=rs, device_id=dev, device_id_type=MESH
        )

    barrier = pltpu.get_barrier_semaphore()
    for k in range(1, nx):
        pl.semaphore_signal(barrier, inc=1, device_id=to_xz(x + k, z), device_id_type=MESH)
    for k in range(1, nz):
        pl.semaphore_signal(barrier, inc=1, device_id=to_xz(x, z + k), device_id_type=MESH)
    for k in range(1, nb):
        pl.semaphore_signal(barrier, inc=1, device_id=to_b(bid + k), device_id_type=MESH)

    load_tp = pltpu.make_async_copy(tp_hbm, tp, local_s.at[0])
    load_sp = pltpu.make_async_copy(sp_hbm, sp, local_s.at[1])
    load_tp.start()
    load_sp.start()

    tall[z, pl.ds(my, rows), :] = unit_rows(tf[...])[0].astype(BF16)
    uall[z, pl.ds(my, rows), :] = unit_rows(sf[...])[0].astype(BF16)
    colacc[...] = jnp.zeros_like(colacc)
    eye = lax.broadcasted_iota(jnp.int32, (LANES, LANES), 0) == lax.broadcasted_iota(
        jnp.int32, (LANES, LANES), 1
    )

    def to_row(col):
        return jnp.sum(jnp.where(eye, col, 0.0), axis=0, keepdims=True)

    def to_col(row):
        return jnp.sum(jnp.where(eye, row, 0.0), axis=1, keepdims=True)

    pl.semaphore_wait(barrier, (nx - 1) + (nz - 1) + (nb - 1))

    half = nz // 2

    def tx(k):
        ref = tall.at[z, pl.ds(my, rows)]
        return remote(ref, ref, tx_s.at[k - 1], tx_r.at[k - 1], to_xz(x + k, z))

    def tright(s):
        ref = tall.at[(z - s + nz) % nz]
        return remote(ref, ref, tr_s.at[s], tr_r.at[s], to_xz(x, z + 1))

    def tleft(s):
        ref = tall.at[(z + s) % nz]
        return remote(ref, ref, tl_s.at[s], tl_r.at[s], to_xz(x, z + nz - 1))

    def uright(s):
        ref = uall.at[(z - s + nz) % nz, pl.ds(my, rows)]
        return remote(ref, ref, ur_s.at[s], ur_r.at[s], to_xz(x, z + 1))

    def uleft(s):
        ref = uall.at[(z + s) % nz, pl.ds(my, rows)]
        return remote(ref, ref, ul_s.at[s], ul_r.at[s], to_xz(x, z + nz - 1))

    def ux(off, k):
        ref = uall.at[(z + off) % nz, pl.ds(my, rows)]
        return remote(
            ref, ref, ux_s.at[off * (nx - 1) + k - 1], ux_r.at[off * (nx - 1) + k - 1], to_xz(x + k, z)
        )

    for k in range(1, nx):
        tx(k).start()
    uright(0).start()
    if half > 1:
        uleft(0).start()
    for k in range(1, nx):
        ux(0, k).start()

    def compute_m(blk):
        row0 = pl.multiple_of(blk * block, block)
        a = tall[blk]
        for j in range(width // tile):
            cols = slice(j * tile, (j + 1) * tile)
            s = jnp.dot(a, tp[:, cols], preferred_element_type=F32)
            v = jnp.exp2(s * (LOG2E / TEACHER_TEMP))
            m[pl.ds(row0, block), cols] = v
            colacc[:, cols] += jnp.sum(v.reshape(block // 8, 8, tile), axis=0)

    for k in range(1, nx):
        tx(k).wait_recv()
    tright(0).start()
    if half > 1:
        tleft(0).start()
    load_tp.wait()
    compute_m(z)

    @pl.loop(0, half)
    def _(s):
        tright(s).wait_recv()

        @pl.when(s < half - 1)
        def _():
            tright(s + 1).start()
            tleft(s).wait_recv()

        @pl.when(s < half - 2)
        def _():
            tleft(s + 1).start()

        uright(s).wait_recv()

        @pl.when(s < half - 1)
        def _():
            uright(s + 1).start()
            uleft(s).wait_recv()

        @pl.when(s < half - 2)
        def _():
            uleft(s + 1).start()

        for k in range(1, nx):
            ux(nz - 1 - s, k).start()

        @pl.when(s < half - 1)
        def _():
            for k in range(1, nx):
                ux(s + 1, k).start()

        @pl.loop(0, jnp.where(s < half - 1, 2, 1))
        def _(k):
            off = jnp.where(k == 0, nz - 1 - s, 1 + s)
            compute_m((z + off) % nz)

    def cb_copy(it, k):
        return remote(
            ps.at[it], cb.at[it, k - 1], cb_s.at[it, k - 1], cb_r.at[it, k - 1], to_b(bid + k)
        )

    def ax_copy(it, k):
        n = groups if it < ITERS - 1 else 2 * groups
        return remote(
            payload.at[it, pl.ds(0, n)], xb.at[it, k - 1, pl.ds(0, n)],
            ax_s.at[it, k - 1], ax_r.at[it, k - 1], to_xz(x + k, z),
        )

    def az_copy(it, k):
        n = groups if it < ITERS - 1 else 2 * groups
        return remote(
            zb_sum.at[it, pl.ds(0, n)], zb.at[it, k - 1, pl.ds(0, n)],
            az_s.at[it, k - 1], az_r.at[it, k - 1], to_xz(x, z + k),
        )

    def compute_e(blk):
        row0 = pl.multiple_of(blk * block, block)
        a = uall[blk]
        acc = jnp.zeros((block, LANES), F32)
        for j in range(width // tile):
            cols = slice(j * tile, (j + 1) * tile)
            s = jnp.dot(a, sp[:, cols], preferred_element_type=F32)
            v = jnp.exp2(jnp.minimum(s * (LOG2E / STUDENT_TEMP) - 2.0, 127.0))
            e[pl.ds(row0, block), cols] = v
            for t in range(tile // LANES):
                acc += v[:, t * LANES : (t + 1) * LANES]
        for i in range(per):
            col = jnp.sum(acc[i * LANES : (i + 1) * LANES], axis=1, keepdims=True)
            payload[ITERS - 1, pl.ds(groups + blk * per + i, 1), :] = to_row(col)

    def e_blocks(lo, hi):
        @pl.loop(lo, hi)
        def _(k):
            compute_e((z + k) % nz)

    def colsum():
        def body(i, acc):
            col = to_col(ccs[pl.ds(i, 1), :])
            for q in range(LANES // 8):
                acc = acc + m[pl.ds(i * LANES + q * 8, 8), :] * col[q * 8 : (q + 1) * 8]
            return acc

        return lax.fori_loop(0, groups, body, jnp.zeros((8, width), F32))

    def rowsum(it, scale):
        @pl.loop(0, groups)
        def _(i):
            acc = jnp.zeros((LANES, LANES), F32)
            for t in range(width // LANES):
                cols = slice(t * LANES, (t + 1) * LANES)
                acc = acc + m[pl.ds(i * LANES, LANES), cols] * scale[:, cols]
            col = jnp.sum(acc, axis=1, keepdims=True)
            payload[it, pl.ds(i, 1), :] = to_row(col)

    cuts = [nz * i // 8 for i in range(9)]
    for it in range(ITERS):
        part = colacc[...] if it == 0 else colsum()
        ps[it] = jnp.sum(part, axis=0, keepdims=True)
        for k in range(1, nb):
            cb_copy(it, k).start()
        if it == 0:
            load_sp.wait()
            for off in range(nz):
                for k in range(1, nx):
                    ux(off, k).wait_recv()
            e_blocks(cuts[0], cuts[2])
        elif it == 1:
            e_blocks(cuts[5], cuts[7])
        else:

            @pl.loop(0, nz)
            def _(k):
                ut[:, pl.ds(pl.multiple_of(k * block, block), block)] = uall[k].T

        for k in range(1, nb):
            cb_copy(it, k).wait_recv()
        total = ps[it]
        for k in range(1, nb):
            total = total + cb[it, k - 1]
        scale = 1.0 / total
        rowsum(it, scale)
        if it == ITERS - 1:
            cps = scale
        for k in range(1, nx):
            ax_copy(it, k).start()
        if it == 0:
            e_blocks(cuts[2], cuts[3])
        elif it == 1:
            e_blocks(cuts[7], cuts[8])
        for k in range(1, nx):
            ax_copy(it, k).wait_recv()
        n = groups if it < ITERS - 1 else 2 * groups
        total = payload[it, pl.ds(0, n)]
        for k in range(1, nx):
            total = total + xb[it, k - 1, pl.ds(0, n)]
        zb_sum[it, pl.ds(0, n)] = total
        for k in range(1, nz):
            az_copy(it, k).start()
        if it == 0:
            e_blocks(cuts[3], cuts[5])
        elif it == 1:

            @pl.loop(0, width // tile)
            def _(j):
                cols = pl.ds(pl.multiple_of(j * tile, tile), tile)
                spt[cols, :] = sp[:, cols].T

        for k in range(1, nz):
            az_copy(it, k).wait_recv()
        total = zb_sum[it, pl.ds(0, n)]
        for k in range(1, nz):
            total = total + zb[it, k - 1, pl.ds(0, n)]
        inverse = 1.0 / total
        ccs[...] = inverse[:groups]
        if it == ITERS - 1:
            cinv[...] = inverse[groups:]

    def order(s):
        return half + jnp.where(s % 2 == 0, s // 2, -((s + 1) // 2))

    def fx_copy(off, k):
        blk = (z + off) % nz
        xx = (x + k) % nx
        return remote(
            ugb.at[blk, pl.ds(pl.multiple_of(xx * rows, rows), rows)],
            xr.at[k - 1, blk],
            fx_s.at[off * (nx - 1) + k - 1], fx_r.at[off * (nx - 1) + k - 1], to_xz(xx, z),
        )

    def fz_copy(off):
        return remote(
            zs.at[off], zr.at[off - 1], fz_s.at[off - 1], fz_r.at[off - 1], to_xz(x, z + off)
        )

    @pl.loop(0, nz)
    def _(s):
        off = order(s)
        blk = (z + off) % nz
        row0 = pl.multiple_of(blk * block, block)
        inv = jnp.concatenate([to_col(cinv[pl.ds(blk * per + i, 1), :]) for i in range(per)], axis=0)
        sca = jnp.concatenate([to_col(ccs[pl.ds(blk * per + i, 1), :]) for i in range(per)], axis=0)
        acc = jnp.zeros((block, depth), F32)
        for j in range(width // tile):
            cols = slice(j * tile, (j + 1) * tile)
            prob = e[pl.ds(row0, block), cols] * inv
            target = (m[pl.ds(row0, block), cols] * sca) * cps[:, cols]
            gh = (prob - target).astype(BF16)
            g[pl.ds(row0, block), cols] = gh
            acc += jnp.dot(gh, spt[cols, :], preferred_element_type=F32)
        ugb[blk] = acc.astype(BF16)
        for k in range(1, nx):
            fx_copy(off, k).start()

    def pc_copy(j):
        cols = pl.ds(pl.multiple_of(j * chunk, chunk), chunk)
        return remote(
            pgb.at[1 - c, :, :, cols], cr.at[:, :, cols], pc_s.at[j], pc_r.at[j], to_b(y * 2 + 1 - c)
        )

    def py_copy(j, k):
        cols = pl.ds(pl.multiple_of(j * chunk, chunk), chunk)
        return remote(
            ys.at[k - 1, :, cols], yr.at[k - 1, :, cols],
            py_s.at[j, k - 1], py_r.at[j, k - 1], to_b(bid + 2 * k),
        )

    @pl.loop(0, width // chunk)
    def _(j):
        cols = pl.ds(pl.multiple_of(j * chunk, chunk), chunk)
        part = jnp.dot(ut[...], g[:, cols], preferred_element_type=F32)
        for yy in range(ny):
            for cc in range(2):
                d0 = (yy * 2 + cc) * dr
                pgf[cc, yy, :, cols] = part[d0 : d0 + dr]
                pgb[cc, yy, :, cols] = part[d0 : d0 + dr].astype(BF16)
        pc_copy(j).start()

    @pl.loop(0, nz)
    def _(s):
        off = order(s)
        blk = (z + off) % nz
        for k in range(1, nx):
            fx_copy(off, k).wait_recv()
        total = ugb[blk, pl.ds(my, rows), :].astype(F32)
        for k in range(1, nx):
            total = total + xr[k - 1, blk].astype(F32)
        zs[off] = total.astype(BF16)

        @pl.when(s < nz - 1)
        def _():
            fz_copy(off).start()

        nch = width // chunk

        @pl.when((s % 2 == 1) & (s // 2 < nch))
        def _():
            j = s // 2
            cols = pl.ds(pl.multiple_of(j * chunk, chunk), chunk)
            pc_copy(j).wait_recv()
            pg_out[:, cols] = pgf[c, y, :, cols] + cr[y, :, cols].astype(F32)
            for k in range(1, ny):
                yy = (y + k) % ny
                ys[k - 1, :, cols] = (pgf[c, yy, :, cols] + cr[yy, :, cols].astype(F32)).astype(BF16)
                py_copy(j, k).start()

    for off in range(1, nz):
        fz_copy(off).wait_recv()
    total = zs[0].astype(F32)
    for off in range(1, nz):
        total = total + zr[off - 1].astype(F32)
    total = total / STUDENT_TEMP
    unit, norm = unit_rows(sf[...])
    inner = jnp.sum(unit * total, axis=1, keepdims=True)
    fg_out[...] = (total - unit * inner) / norm

    @pl.loop(0, width // chunk)
    def _(j):
        cols = pl.ds(pl.multiple_of(j * chunk, chunk), chunk)
        total = pg_out[:, cols]
        for k in range(1, ny):
            py_copy(j, k).wait_recv()
            total = total + yr[k - 1, :, cols].astype(F32)
        pg_out[:, cols] = total / STUDENT_TEMP

    for k in range(1, nx):
        tx(k).wait_send()

    @pl.loop(0, half)
    def _(s):
        tright(s).wait_send()
        uright(s).wait_send()

        @pl.when(s < half - 1)
        def _():
            tleft(s).wait_send()
            uleft(s).wait_send()

    @pl.loop(0, nz)
    def _(off):
        for k in range(1, nx):
            ux(off, k).wait_send()
            fx_copy(off, k).wait_send()

        @pl.when(off > 0)
        def _():
            fz_copy(off).wait_send()

    for it in range(ITERS):
        for k in range(1, nb):
            cb_copy(it, k).wait_send()
        for k in range(1, nx):
            ax_copy(it, k).wait_send()
        for k in range(1, nz):
            az_copy(it, k).wait_send()

    @pl.loop(0, width // chunk)
    def _(j):
        pc_copy(j).wait_send()
        for k in range(1, ny):
            py_copy(j, k).wait_send()


def shards(nx, nz, ny, student_feats, teacher_feats, student_protos, teacher_protos):
    rows, depth = student_feats.shape
    width = student_protos.shape[1]
    block, nb = nx * rows, 2 * ny
    crops, dr = nz * block, depth // nb
    groups = crops // LANES
    chunk = min(512, width)
    nch = width // chunk
    half = nz // 2
    one = lambda n: max(n, 1)
    x1, y1, z1, b1 = one(nx - 1), one(ny - 1), one(nz - 1), nb - 1
    dma = pltpu.SemaphoreType.DMA
    vmem = pl.BlockSpec(memory_space=pltpu.VMEM)
    hbm = pl.BlockSpec(memory_space=pl.ANY)
    scratch = [
        pltpu.VMEM((depth, width), BF16),
        pltpu.VMEM((depth, width), BF16),
        pltpu.VMEM((width, depth), BF16),
        pltpu.VMEM((nz, block, depth), BF16),
        pltpu.VMEM((nz, block, depth), BF16),
        pltpu.VMEM((depth, crops), BF16),
        pltpu.VMEM((crops, width), F32),
        pltpu.VMEM((crops, width), F32),
        pltpu.VMEM((crops, width), BF16),
        pltpu.VMEM((8, width), F32),
        pltpu.VMEM((ITERS, 1, width), F32),
        pltpu.VMEM((ITERS, 2 * groups, LANES), F32),
        pltpu.VMEM((groups, LANES), F32),
        pltpu.VMEM((groups, LANES), F32),
        pltpu.VMEM((ITERS, b1, 1, width), F32),
        pltpu.VMEM((ITERS, x1, 2 * groups, LANES), F32),
        pltpu.VMEM((ITERS, 2 * groups, LANES), F32),
        pltpu.VMEM((ITERS, z1, 2 * groups, LANES), F32),
        pltpu.VMEM((nz, block, depth), BF16),
        pltpu.VMEM((x1, nz, rows, depth), BF16),
        pltpu.VMEM((nz, rows, depth), BF16),
        pltpu.VMEM((z1, rows, depth), BF16),
        pltpu.VMEM((2, ny, dr, width), F32),
        pltpu.VMEM((2, ny, dr, width), BF16),
        pltpu.VMEM((ny, dr, width), BF16),
        pltpu.VMEM((y1, dr, width), BF16),
        pltpu.VMEM((y1, dr, width), BF16),
        dma((2,)),
        dma((x1,)), dma((x1,)), dma((half,)), dma((half,)), dma((half,)), dma((half,)),
        dma((half,)), dma((half,)), dma((half,)), dma((half,)), dma((nz * x1,)), dma((nz * x1,)),
        dma((ITERS, b1)), dma((ITERS, b1)), dma((ITERS, x1)), dma((ITERS, x1)),
        dma((ITERS, z1)), dma((ITERS, z1)),
        dma((nz * x1,)), dma((nz * x1,)), dma((z1,)), dma((z1,)),
        dma((nch,)), dma((nch,)), dma((nch, y1)), dma((nch, y1)),
    ]
    return pl.pallas_call(
        functools.partial(kernel, nx, nz, ny),
        out_shape=(
            jax.ShapeDtypeStruct((dr, width), F32),
            jax.ShapeDtypeStruct((rows, depth), F32),
        ),
        in_specs=[vmem, vmem, hbm, hbm],
        out_specs=(vmem, vmem),
        scratch_shapes=scratch,
        compiler_params=pltpu.CompilerParams(
            collective_id=0, has_side_effects=True, vmem_limit_bytes=60 * 1024 * 1024
        ),
        cost_estimate=pl.CostEstimate(
            flops=8 * crops * width * depth, bytes_accessed=4 * depth * width,
            transcendentals=2 * crops * width,
        ),
    )(student_feats, teacher_feats, student_protos, teacher_protos)


def solution(mesh, nz=8):
    nx, ny = mesh.shape["proto"] // nz, mesh.shape["batch"] // 2
    in_specs = (
        P(("batch", "proto"), None),
        P(("batch", "proto"), None),
        P(None, "proto"),
        P(None, "proto"),
    )
    out_specs = (P("batch", "proto"), P(("batch", "proto"), None))
    return jax.shard_map(
        functools.partial(shards, nx, nz, ny),
        mesh=mesh, in_specs=in_specs, out_specs=out_specs, check_vma=False,
    )
```

```python
import functools

import jax
import jax.numpy as jnp
from jax import lax
from jax.experimental import pallas as pl
from jax.experimental.pallas import tpu as pltpu
from jax.sharding import PartitionSpec as P

ITERS = 3
STUDENT_TEMP = 0.1
TEACHER_TEMP = 0.07
LOG2E = 1.4426950408889634
MESH = pl.DeviceIdType.MESH
F32 = jnp.float32
BF16 = jnp.bfloat16
LANES = 128


def unit_rows(feats):
    values = feats.astype(F32)
    norm = jnp.sqrt(jnp.sum(values * values, axis=1, keepdims=True) + 1e-06)
    return values / norm, norm


def kernel(
    nx, nz, ny,
    sf, tf, sp_hbm, tp_hbm,
    pg_out, fg_out,
    tp, sp, spt, tall, uall, ut, m, e, g,
    colacc, ps, lse_acc, pay, cinv, ccs,
    cb, pb,
    ugb, ug0, near, xr, zs, zr,
    pgf, pgb, cr, ys, yr,
    local_s,
    tz_s, tz_r, tx_s, tx_r, uz_s, uz_r, ux_s, ux_r,
    cb_s, cb_r, pb_s, pb_r,
    fn_s, fn_r, fx_s, fx_r, fz_s, fz_r, pc_s, pc_r, py_s, py_r,
):
    rows = sf.shape[0]
    depth, width = tp.shape
    block = nx * rows
    crops = nz * block
    nb = 2 * ny
    dr = depth // nb
    tile = min(256, width)
    groups = crops // LANES
    per = block // LANES
    chunk = min(512, width)

    pid = lax.axis_index("proto")
    bid = lax.axis_index("batch")
    x, z = pid // nz, pid % nz
    y, c = bid // 2, bid % 2
    my = pl.multiple_of(x * rows, rows)

    def to_xz(xx, zz):
        return {"proto": (xx % nx) * nz + zz % nz}

    def to_b(bb):
        return {"batch": bb % nb}

    def remote(src, dst, ss, rs, dev):
        return pltpu.make_async_remote_copy(
            src_ref=src, dst_ref=dst, send_sem=ss, recv_sem=rs, device_id=dev, device_id_type=MESH
        )

    drain = []

    barrier = pltpu.get_barrier_semaphore()
    for kx in range(nx):
        for kz in range(nz):
            if kx or kz:
                pl.semaphore_signal(
                    barrier, inc=1, device_id=to_xz(x + kx, z + kz), device_id_type=MESH
                )
    for k in range(1, nb):
        pl.semaphore_signal(barrier, inc=1, device_id=to_b(bid + k), device_id_type=MESH)

    load_tp = pltpu.make_async_copy(tp_hbm, tp, local_s.at[0])
    load_sp = pltpu.make_async_copy(sp_hbm, sp, local_s.at[1])
    load_tp.start()
    load_sp.start()

    tall[z, pl.ds(my, rows), :] = unit_rows(tf[...])[0].astype(BF16)
    uall[z, pl.ds(my, rows), :] = unit_rows(sf[...])[0].astype(BF16)
    colacc[...] = jnp.zeros_like(colacc)
    eye = lax.broadcasted_iota(jnp.int32, (LANES, LANES), 0) == lax.broadcasted_iota(
        jnp.int32, (LANES, LANES), 1
    )

    def to_row(col):
        return jnp.sum(jnp.where(eye, col, 0.0), axis=0, keepdims=True)

    def to_col(row):
        return jnp.sum(jnp.where(eye, row, 0.0), axis=1, keepdims=True)

    pl.semaphore_wait(barrier, (nx * nz - 1) + (nb - 1))

    near_z = sorted({1, nz - 1})
    far_z = [d for d in range(1, nz) if d not in near_z]
    far_z = sorted(far_z, key=lambda d: (min(d, nz - d), d))

    def tz(d):
        ref = tall.at[z, pl.ds(my, rows)]
        return remote(ref, ref, tz_s.at[d], tz_r.at[d], to_xz(x, z + d))

    def trow(d):
        ref = tall.at[z]
        return remote(ref, ref, tz_s.at[d], tz_r.at[d], to_xz(x, z + d))

    def tx(d, k):
        ref = tall.at[(z + nz - d) % nz, pl.ds(my, rows)]
        i = d * (nx - 1) + k - 1
        return remote(ref, ref, tx_s.at[i], tx_r.at[i], to_xz(x + k, z))

    def uz(d):
        ref = uall.at[z, pl.ds(my, rows)]
        return remote(ref, ref, uz_s.at[d], uz_r.at[d], to_xz(x, z + d))

    def ux(d, k):
        ref = uall.at[(z + nz - d) % nz, pl.ds(my, rows)]
        i = d * (nx - 1) + k - 1
        return remote(ref, ref, ux_s.at[i], ux_r.at[i], to_xz(x + k, z))

    for k in range(1, nx):
        tx(0, k).start()
    for d in far_z:
        tz(d).start()

    def compute_m(blk):
        row0 = pl.multiple_of(blk * block, block)
        a = tall[blk]
        for j in range(width // tile):
            cols = slice(j * tile, (j + 1) * tile)
            s = jnp.dot(a, tp[:, cols], preferred_element_type=F32)
            v = jnp.exp2(s * (LOG2E / TEACHER_TEMP))
            m[pl.ds(row0, block), cols] = v
            colacc[:, cols] += jnp.sum(v.reshape(block // 8, 8, tile), axis=0)

    for k in range(1, nx):
        tx(0, k).wait_recv()
    for d in near_z:
        trow(d).start()
    load_tp.wait()
    compute_m(z)
    for d in far_z:
        tz(d).wait_recv()
        for k in range(1, nx):
            tx(d, k).start()
    for k in range(1, nx):
        ux(0, k).start()
    for d in range(1, nz):
        uz(d).start()

    def pick(s, table):
        out = jnp.int32(table[0])
        for i in range(1, len(table)):
            out = jnp.where(s == i, table[i], out)
        return out

    arrivals = far_z[:2] + near_z + far_z[2:]

    @pl.loop(0, nz - 1)
    def _(s):
        d = pick(s, arrivals)
        is_near = (d == 1) | (d == nz - 1)

        @pl.when(is_near)
        def _():
            trow(d).wait_recv()

        @pl.when(jnp.logical_not(is_near))
        def _():
            for k in range(1, nx):
                tx(d, k).wait_recv()

        compute_m((z + nz - d) % nz)

    def gathered():
        for k in range(1, nx):
            tx(0, k).wait_send()
        for d in near_z:
            trow(d).wait_send()
        for d in far_z:
            tz(d).wait_send()
            for k in range(1, nx):
                tx(d, k).wait_send()

    drain.append(gathered)

    def cb_copy(it, k):
        return remote(
            ps.at[it], cb.at[it, k - 1], cb_s.at[it, k - 1], cb_r.at[it, k - 1], to_b(bid + k)
        )

    def pb_copy(it, kx, kz):
        i = kx * nz + kz - 1
        return remote(
            pay.at[it], pb.at[it, i], pb_s.at[it, i], pb_r.at[it, i], to_xz(x + kx, z + kz)
        )

    others = [(kx, kz) for kx in range(nx) for kz in range(nz) if kx or kz]

    def pb_total(it):
        total = pay[it].astype(F32)
        for i in range(nx * nz - 1):
            total = total + pb[it, i].astype(F32)
        return total

    def compute_e(blk):
        row0 = pl.multiple_of(blk * block, block)
        a = uall[blk]
        acc = jnp.zeros((block, LANES), F32)
        for j in range(width // tile):
            cols = slice(j * tile, (j + 1) * tile)
            s = jnp.dot(a, sp[:, cols], preferred_element_type=F32)
            v = jnp.exp2(jnp.minimum(s * (LOG2E / STUDENT_TEMP) - 2.0, 127.0))
            e[pl.ds(row0, block), cols] = v
            for t in range(tile // LANES):
                acc += v[:, t * LANES : (t + 1) * LANES]
        for i in range(per):
            col = jnp.sum(acc[i * LANES : (i + 1) * LANES], axis=1, keepdims=True)
            lse_acc[pl.ds(blk * per + i, 1), :] = to_row(col)

    def e_blocks(ds):
        @pl.loop(0, len(ds))
        def _(s):
            d = pick(s, ds)
            for k in range(1, nx):
                ux(d, k).wait_recv()
            compute_e((z + nz - d) % nz)

    def u_forward(ds):
        for d in ds:
            uz(d).wait_recv()
            for k in range(1, nx):
                ux(d, k).start()

    def colsum():
        def body(i, acc):
            col = to_col(ccs[pl.ds(i, 1), :])
            for q in range(LANES // 8):
                acc = acc + m[pl.ds(i * LANES + q * 8, 8), :] * col[q * 8 : (q + 1) * 8]
            return acc

        return lax.fori_loop(0, groups, body, jnp.zeros((8, width), F32), unroll=min(4, groups))

    def rowsum(scale):
        def body(i):
            acc = jnp.zeros((LANES, LANES), F32)
            for t in range(width // LANES):
                cols = slice(t * LANES, (t + 1) * LANES)
                acc = acc + m[pl.ds(i * LANES, LANES), cols] * scale[:, cols]
            ccs[pl.ds(i, 1), :] = to_row(jnp.sum(acc, axis=1, keepdims=True))

        pl.loop(0, groups, unroll=min(4, groups))(body)

    u_order = [d for d in range(1, nz)]
    cut = (len(u_order) - 1) // 2
    for it in range(ITERS):
        part = colacc[...] if it == 0 else colsum()
        ps[it] = jnp.sum(part, axis=0, keepdims=True)
        for k in range(1, nb):
            cb_copy(it, k).start()
        if it == 0:
            load_sp.wait()

            @pl.loop(0, width // tile)
            def _(j):
                cols = pl.ds(pl.multiple_of(j * tile, tile), tile)
                spt[cols, :] = sp[:, cols].T

        elif it == 1:
            u_forward(u_order[cut:])
            e_blocks(u_order[:cut])
        else:
            pay[ITERS] = lse_acc[...].astype(BF16)
            for kx, kz in others:
                pb_copy(ITERS, kx, kz).start()

            @pl.loop(0, nz)
            def _(k):
                ut[:, pl.ds(pl.multiple_of(k * block, block), block)] = uall[k].T

        for k in range(1, nb):
            cb_copy(it, k).wait_recv()
        total = ps[it]
        for k in range(1, nb):
            total = total + cb[it, k - 1]
        scale = 1.0 / total
        if it == 0:
            u_forward(u_order[:cut])
        rowsum(scale)
        if it == ITERS - 1:
            cps = scale
        pay[it] = ccs[...].astype(BF16)
        for kx, kz in others:
            pb_copy(it, kx, kz).start()
        if it == 0:
            e_blocks([0])
        elif it == 1:
            e_blocks(u_order[cut:])
        else:
            for kx, kz in others:
                pb_copy(ITERS, kx, kz).wait_recv()
            cinv[...] = 1.0 / pb_total(ITERS)
        for kx, kz in others:
            pb_copy(it, kx, kz).wait_recv()
        ccs[...] = 1.0 / pb_total(it)

        def reduced(it=it):
            for k in range(1, nb):
                cb_copy(it, k).wait_send()
            for kx, kz in others:
                pb_copy(it, kx, kz).wait_send()

        drain.append(reduced)

    def student():
        for k in range(1, nx):
            ux(0, k).wait_send()
        for d in range(1, nz):
            uz(d).wait_send()
            for k in range(1, nx):
                ux(d, k).wait_send()
        for kx, kz in others:
            pb_copy(ITERS, kx, kz).wait_send()

    drain.append(student)

    def fn_copy(d):
        i = near_z.index(d)
        return remote(
            ugb.at[(z + d) % nz], near.at[i], fn_s.at[i], fn_r.at[i], to_xz(x, z + d)
        )

    def fx_copy(d, k):
        xx = (x + k) % nx
        i = d * (nx - 1) + k - 1
        return remote(
            ugb.at[(z + d) % nz, pl.ds(pl.multiple_of(xx * rows, rows), rows)],
            xr.at[k - 1, d], fx_s.at[i], fx_r.at[i], to_xz(xx, z),
        )

    def fz_copy(d):
        return remote(zs.at[d], zr.at[d], fz_s.at[d], fz_r.at[d], to_xz(x, z + d))

    late = far_z[::-1]
    series = near_z + late + [0]
    pairs = [series[i : i + 2] for i in range(0, nz, 2)]

    @pl.loop(0, len(pairs))
    def _(s):
        blks = [(z + pick(s, [p[i] for p in pairs])) % nz for i in range(2)]
        invs, scas = [
            [
                jnp.concatenate([to_col(ref[pl.ds(blk * per + i, 1), :]) for i in range(per)], axis=0)
                for blk in blks
            ]
            for ref in (cinv, ccs)
        ]
        acc = jnp.zeros((2 * block, depth), F32)
        for j in range(width // tile):
            cols = slice(j * tile, (j + 1) * tile)
            both = []
            for blk, inv, sca in zip(blks, invs, scas):
                at = pl.ds(pl.multiple_of(blk * block, block), block)
                prob = e[at, cols] * inv
                target = (m[at, cols] * sca) * cps[:, cols]
                gh = (prob - target).astype(BF16)
                g[at, cols] = gh
                both.append(gh)
            acc += jnp.dot(jnp.concatenate(both, axis=0), spt[cols, :], preferred_element_type=F32)
        for i, blk in enumerate(blks):
            ugb[blk] = acc[i * block : (i + 1) * block].astype(BF16)

        @pl.when(s == len(pairs) - 1)
        def _():
            ug0[...] = acc[block:]

        for i, p in enumerate(pairs):

            @pl.when(s == i)
            def _():
                for d in p:
                    if d in near_z:
                        fn_copy(d).start()
                    elif d:
                        for k in range(1, nx):
                            fx_copy(d, k).start()

    nch = width // chunk

    def pc_copy(j):
        cols = pl.ds(pl.multiple_of(j * chunk, chunk), chunk)
        return remote(
            pgb.at[1 - c, :, :, cols], cr.at[:, :, cols], pc_s.at[j], pc_r.at[j], to_b(y * 2 + 1 - c)
        )

    def py_copy(j, k):
        cols = pl.ds(pl.multiple_of(j * chunk, chunk), chunk)
        return remote(
            ys.at[k - 1, :, cols], yr.at[k - 1, :, cols],
            py_s.at[j, k - 1], py_r.at[j, k - 1], to_b(bid + 2 * k),
        )

    def pc_sum(j):
        cols = pl.ds(pl.multiple_of(j * chunk, chunk), chunk)
        pc_copy(j).wait_recv()
        for k in range(1, ny):
            yy = (y + k) % ny
            ys[k - 1, :, cols] = (pgf[c, yy, :, cols] + cr[yy, :, cols].astype(F32)).astype(BF16)
            py_copy(j, k).start()
        pg_out[:, cols] = pgf[c, y, :, cols] + cr[y, :, cols].astype(F32)

    @pl.loop(0, nch)
    def _(j):
        cols = pl.ds(pl.multiple_of(j * chunk, chunk), chunk)
        part = jnp.dot(ut[...], g[:, cols], preferred_element_type=F32)
        for yy in range(ny):
            for cc in range(2):
                d0 = (yy * 2 + cc) * dr
                pgf[cc, yy, :, cols] = part[d0 : d0 + dr]
                pgb[cc, yy, :, cols] = part[d0 : d0 + dr].astype(BF16)
        pc_copy(j).start()

        @pl.when(j > 0)
        def _():
            pc_sum(j - 1)

        @pl.when(j == min(1, nch - 1))
        def _():
            total = ug0[...]
            for i, d in enumerate(near_z):
                fn_copy(d).wait_recv()
                total = total + near[i].astype(F32)
            ug0[...] = total
            ugb[z] = total.astype(BF16)
            for k in range(1, nx):
                fx_copy(0, k).start()

    def x_sum(d):
        for k in range(1, nx):
            fx_copy(d, k).wait_recv()
        total = ugb[(z + d) % nz, pl.ds(my, rows), :].astype(F32) if d else ug0[pl.ds(my, rows), :]
        for k in range(1, nx):
            total = total + xr[k - 1, d].astype(F32)
        return total

    for i, d in enumerate(late):
        zs[d] = x_sum(d).astype(BF16)
        fz_copy(d).start()
        if i == 0:
            pc_sum(nch - 1)
    if not late:
        pc_sum(nch - 1)
    total = x_sum(0)
    for d in late:
        fz_copy(d).wait_recv()
        total = total + zr[d].astype(F32)
    total = total / STUDENT_TEMP
    unit, norm = unit_rows(sf[...])
    inner = jnp.sum(unit * total, axis=1, keepdims=True)
    fg_out[...] = (total - unit * inner) / norm

    @pl.loop(0, nch)
    def _(j):
        cols = pl.ds(pl.multiple_of(j * chunk, chunk), chunk)
        total = pg_out[:, cols]
        for k in range(1, ny):
            py_copy(j, k).wait_recv()
            total = total + yr[k - 1, :, cols].astype(F32)
        pg_out[:, cols] = total / STUDENT_TEMP

    def grads():
        for d in near_z:
            fn_copy(d).wait_send()
        for d in late + [0]:
            for k in range(1, nx):
                fx_copy(d, k).wait_send()
        for d in late:
            fz_copy(d).wait_send()

        @pl.loop(0, nch)
        def _(j):
            pc_copy(j).wait_send()
            for k in range(1, ny):
                py_copy(j, k).wait_send()

    drain.append(grads)
    for leave in drain:
        leave()


def shards(nx, nz, ny, student_feats, teacher_feats, student_protos, teacher_protos):
    rows, depth = student_feats.shape
    width = student_protos.shape[1]
    block, nb = nx * rows, 2 * ny
    crops, dr = nz * block, depth // nb
    groups = crops // LANES
    chunk = min(512, width)
    nch = width // chunk
    one = lambda n: max(n, 1)
    x1, y1, b1 = one(nx - 1), one(ny - 1), nb - 1
    dma = pltpu.SemaphoreType.DMA
    vmem = pl.BlockSpec(memory_space=pltpu.VMEM)
    hbm = pl.BlockSpec(memory_space=pl.ANY)
    scratch = [
        pltpu.VMEM((depth, width), BF16),
        pltpu.VMEM((depth, width), BF16),
        pltpu.VMEM((width, depth), BF16),
        pltpu.VMEM((nz, block, depth), BF16),
        pltpu.VMEM((nz, block, depth), BF16),
        pltpu.VMEM((depth, crops), BF16),
        pltpu.VMEM((crops, width), F32),
        pltpu.VMEM((crops, width), F32),
        pltpu.VMEM((crops, width), BF16),
        pltpu.VMEM((8, width), F32),
        pltpu.VMEM((ITERS, 1, width), F32),
        pltpu.VMEM((groups, LANES), F32),
        pltpu.VMEM((ITERS + 1, groups, LANES), BF16),
        pltpu.VMEM((groups, LANES), F32),
        pltpu.VMEM((groups, LANES), F32),
        pltpu.VMEM((ITERS, b1, 1, width), F32),
        pltpu.VMEM((ITERS + 1, nx * nz - 1, groups, LANES), BF16),
        pltpu.VMEM((nz, block, depth), BF16),
        pltpu.VMEM((block, depth), F32),
        pltpu.VMEM((2, block, depth), BF16),
        pltpu.VMEM((x1, nz, rows, depth), BF16),
        pltpu.VMEM((nz, rows, depth), BF16),
        pltpu.VMEM((nz, rows, depth), BF16),
        pltpu.VMEM((2, ny, dr, width), F32),
        pltpu.VMEM((2, ny, dr, width), BF16),
        pltpu.VMEM((ny, dr, width), BF16),
        pltpu.VMEM((y1, dr, width), BF16),
        pltpu.VMEM((y1, dr, width), BF16),
        dma((2,)),
        dma((nz,)), dma((nz,)), dma((nz * x1,)), dma((nz * x1,)),
        dma((nz,)), dma((nz,)), dma((nz * x1,)), dma((nz * x1,)),
        dma((ITERS, b1)), dma((ITERS, b1)),
        dma((ITERS + 1, nx * nz - 1)), dma((ITERS + 1, nx * nz - 1)),
        dma((2,)), dma((2,)), dma((nz * x1,)), dma((nz * x1,)), dma((nz,)), dma((nz,)),
        dma((nch,)), dma((nch,)), dma((nch, y1)), dma((nch, y1)),
    ]
    return pl.pallas_call(
        functools.partial(kernel, nx, nz, ny),
        out_shape=(
            jax.ShapeDtypeStruct((dr, width), F32),
            jax.ShapeDtypeStruct((rows, depth), F32),
        ),
        in_specs=[vmem, vmem, hbm, hbm],
        out_specs=(vmem, vmem),
        scratch_shapes=scratch,
        compiler_params=pltpu.CompilerParams(
            collective_id=0, has_side_effects=True, vmem_limit_bytes=60 * 1024 * 1024
        ),
        cost_estimate=pl.CostEstimate(
            flops=8 * crops * width * depth, bytes_accessed=4 * depth * width,
            transcendentals=2 * crops * width,
        ),
    )(student_feats, teacher_feats, student_protos, teacher_protos)


def solution(mesh, nz=8):
    nx, ny = mesh.shape["proto"] // nz, mesh.shape["batch"] // 2
    in_specs = (
        P(("batch", "proto"), None),
        P(("batch", "proto"), None),
        P(None, "proto"),
        P(None, "proto"),
    )
    out_specs = (P("batch", "proto"), P(("batch", "proto"), None))
    return jax.shard_map(
        functools.partial(shards, nx, nz, ny),
        mesh=mesh, in_specs=in_specs, out_specs=out_specs, check_vma=False,
    )
```

```python
import functools

import jax
import jax.numpy as jnp
from jax import lax
from jax.experimental import pallas as pl
from jax.experimental.pallas import tpu as pltpu
from jax.sharding import PartitionSpec as P

ITERS = 3
STUDENT_TEMP = 0.1
TEACHER_TEMP = 0.07
LOG2E = 1.4426950408889634
MESH = pl.DeviceIdType.MESH
F32 = jnp.float32
BF16 = jnp.bfloat16
LANES = 128


def unit_rows(feats):
    values = feats.astype(F32)
    norm = jnp.sqrt(jnp.sum(values * values, axis=1, keepdims=True) + 1e-06)
    return values / norm, norm


def kernel(
    nx, nz, ny,
    sf, tf, sp_hbm, tp_hbm,
    pg_out, fg_out,
    tp, sp, spt, tall, uall, ut, m, e, g,
    colacc, ps, lse_acc, pay, cinv, ccs,
    cb, pb,
    ugb, ug0, near, xr, zs, zr,
    pgf, pgb, cr, ys, yr,
    local_s,
    tz_r, tx_r, uz_r, ux_r, cb_r, pb_r, fn_r, fx_r, fz_r, pc_r, py_r,
    t_s, u_s, cb_s, pb_s, f_s, p_s,
    spare,
):
    rows = sf.shape[0]
    depth, width = tp.shape
    block = nx * rows
    crops = nz * block
    nb = 2 * ny
    dr = depth // nb
    tile = min(256, width)
    groups = crops // LANES
    per = block // LANES
    chunk = min(512, width)

    pid = lax.axis_index("proto")
    bid = lax.axis_index("batch")
    x, z = pid // nz, pid % nz
    y, c = bid // 2, bid % 2
    my = pl.multiple_of(x * rows, rows)

    def to_xz(xx, zz):
        return {"proto": (xx % nx) * nz + zz % nz}

    def to_b(bb):
        return {"batch": bb % nb}

    def remote(src, dst, ss, rs, dev):
        return pltpu.make_async_remote_copy(
            src_ref=src, dst_ref=dst, send_sem=ss, recv_sem=rs, device_id=dev, device_id_type=MESH
        )

    drain = []

    row_bytes = rows * depth * 2

    def landed(sem, count):
        if count:
            ref = spare.at[pl.ds(0, count)]
            remote(ref, ref, sem, sem, to_xz(x, z + 1)).wait_recv()

    def gone(sem, count):
        if count:
            ref = spare.at[pl.ds(0, count)]
            remote(ref, ref, sem, sem, to_xz(x, z + 1)).wait_send()

    barrier = pltpu.get_barrier_semaphore()
    for k in range(1, nx):
        pl.semaphore_signal(barrier, inc=1, device_id=to_xz(x + k, z), device_id_type=MESH)
    for k in range(1, nz):
        pl.semaphore_signal(barrier, inc=1, device_id=to_xz(x, z + k), device_id_type=MESH)
    for k in range(1, nb):
        pl.semaphore_signal(barrier, inc=1, device_id=to_b(bid + k), device_id_type=MESH)

    load_tp = pltpu.make_async_copy(tp_hbm, tp, local_s.at[0])
    load_sp = pltpu.make_async_copy(sp_hbm, sp, local_s.at[1])
    load_tp.start()
    load_sp.start()

    tall[z, pl.ds(my, rows), :] = unit_rows(tf[...])[0].astype(BF16)
    uall[z, pl.ds(my, rows), :] = unit_rows(sf[...])[0].astype(BF16)
    colacc[...] = jnp.zeros_like(colacc)
    eye = lax.broadcasted_iota(jnp.int32, (LANES, LANES), 0) == lax.broadcasted_iota(
        jnp.int32, (LANES, LANES), 1
    )

    def to_row(col):
        return jnp.sum(jnp.where(eye, col, 0.0), axis=0, keepdims=True)

    def to_col(row):
        return jnp.sum(jnp.where(eye, row, 0.0), axis=1, keepdims=True)

    pl.semaphore_wait(barrier, (nx - 1) + (nz - 1) + (nb - 1))

    near_z = sorted({1, nz - 1})
    far_z = [d for d in range(1, nz) if d not in near_z]
    far_z = sorted(far_z, key=lambda d: (min(d, nz - d), d))

    u_order = [d for d in range(1, nz)]
    cut = (len(u_order) - 1) // 2
    u_first, u_second = u_order[:cut], u_order[cut:]

    def tz(d):
        ref = tall.at[z, pl.ds(my, rows)]
        return remote(ref, ref, t_s, tz_r.at[d], to_xz(x, z + d))

    def trow(d):
        ref = tall.at[z]
        return remote(ref, ref, t_s, tz_r.at[d], to_xz(x, z + d))

    def tx(d, k):
        ref = tall.at[(z + nz - d) % nz, pl.ds(my, rows)]
        return remote(ref, ref, t_s, tx_r.at[d], to_xz(x + k, z))

    def uz(d):
        ref = uall.at[z, pl.ds(my, rows)]
        return remote(ref, ref, u_s, uz_r.at[0 if d in u_first else 1], to_xz(x, z + d))

    def ux(d, k):
        ref = uall.at[(z + nz - d) % nz, pl.ds(my, rows)]
        return remote(ref, ref, u_s, ux_r.at[d], to_xz(x + k, z))

    for k in range(1, nx):
        tx(0, k).start()
    for d in far_z:
        tz(d).start()

    def compute_m(blk):
        row0 = pl.multiple_of(blk * block, block)
        a = tall[blk]
        for j in range(width // tile):
            cols = slice(j * tile, (j + 1) * tile)
            s = jnp.dot(a, tp[:, cols], preferred_element_type=F32)
            v = jnp.exp2(s * (LOG2E / TEACHER_TEMP))
            m[pl.ds(row0, block), cols] = v
            colacc[:, cols] += jnp.sum(v.reshape(block // 8, 8, tile), axis=0)

    landed(tx_r.at[0], nx - 1)
    for d in near_z:
        trow(d).start()
    load_tp.wait()
    compute_m(z)
    for d in far_z:
        tz(d).wait_recv()
        for k in range(1, nx):
            tx(d, k).start()
    for k in range(1, nx):
        ux(0, k).start()
    for d in range(1, nz):
        uz(d).start()

    def pick(s, table):
        out = jnp.int32(table[0])
        for i in range(1, len(table)):
            out = jnp.where(s == i, table[i], out)
        return out

    arrivals = far_z[:2] + near_z + far_z[2:]

    @pl.loop(0, nz - 1)
    def _(s):
        d = pick(s, arrivals)
        is_near = (d == 1) | (d == nz - 1)

        @pl.when(is_near)
        def _():
            trow(d).wait_recv()

        @pl.when(jnp.logical_not(is_near))
        def _():
            landed(tx_r.at[d], nx - 1)

        compute_m((z + nz - d) % nz)

    drain.append(lambda: gone(t_s, (nx - 1) * (1 + len(far_z)) + len(far_z) + nx * len(near_z)))

    def cb_copy(it, k):
        return remote(
            ps.at[it], cb.at[it, k - 1], cb_s, cb_r.at[it], to_b(bid + k)
        )

    def pb_copy(it, kx, kz):
        i = kx * nz + kz - 1
        return remote(
            pay.at[it], pb.at[it, i], pb_s, pb_r.at[it], to_xz(x + kx, z + kz)
        )

    others = [(kx, kz) for kx in range(nx) for kz in range(nz) if kx or kz]

    def pb_landed(it):
        remote(pb.at[it], pb.at[it], pb_s, pb_r.at[it], to_xz(x, z + 1)).wait_recv()

    def pb_total(it):
        total = pay[it].astype(F32)
        for i in range(nx * nz - 1):
            total = total + pb[it, i].astype(F32)
        return total

    def compute_e(blk):
        row0 = pl.multiple_of(blk * block, block)
        a = uall[blk]
        acc = jnp.zeros((block, LANES), F32)
        for j in range(width // tile):
            cols = slice(j * tile, (j + 1) * tile)
            s = jnp.dot(a, sp[:, cols], preferred_element_type=F32)
            v = jnp.exp2(jnp.minimum(s * (LOG2E / STUDENT_TEMP) - 2.0, 127.0))
            e[pl.ds(row0, block), cols] = v
            for t in range(tile // LANES):
                acc += v[:, t * LANES : (t + 1) * LANES]
        for i in range(per):
            col = jnp.sum(acc[i * LANES : (i + 1) * LANES], axis=1, keepdims=True)
            lse_acc[pl.ds(blk * per + i, 1), :] = to_row(col)

    def e_blocks(ds):
        @pl.loop(0, len(ds))
        def _(s):
            d = pick(s, ds)
            landed(ux_r.at[d], nx - 1)
            compute_e((z + nz - d) % nz)

    def u_forward(ds, i):
        landed(uz_r.at[i], len(ds))
        for d in ds:
            for k in range(1, nx):
                ux(d, k).start()

    def colsum():
        def body(i, acc):
            col = to_col(ccs[pl.ds(i, 1), :])
            for q in range(LANES // 8):
                acc = acc + m[pl.ds(i * LANES + q * 8, 8), :] * col[q * 8 : (q + 1) * 8]
            return acc

        return lax.fori_loop(0, groups, body, jnp.zeros((8, width), F32), unroll=min(4, groups))

    def rowsum(scale):
        def body(i):
            acc = jnp.zeros((LANES, LANES), F32)
            for t in range(width // LANES):
                cols = slice(t * LANES, (t + 1) * LANES)
                acc = acc + m[pl.ds(i * LANES, LANES), cols] * scale[:, cols]
            ccs[pl.ds(i, 1), :] = to_row(jnp.sum(acc, axis=1, keepdims=True))

        pl.loop(0, groups, unroll=min(4, groups))(body)

    for it in range(ITERS):
        part = colacc[...] if it == 0 else colsum()
        ps[it] = jnp.sum(part, axis=0, keepdims=True)
        for k in range(1, nb):
            cb_copy(it, k).start()
        if it == 0:
            load_sp.wait()

            @pl.loop(0, width // tile)
            def _(j):
                cols = pl.ds(pl.multiple_of(j * tile, tile), tile)
                spt[cols, :] = sp[:, cols].T

        elif it == 1:
            u_forward(u_second, 1)
            e_blocks(u_first)
        else:
            pay[ITERS] = lse_acc[...].astype(BF16)
            for kx, kz in others:
                pb_copy(ITERS, kx, kz).start()

            @pl.loop(0, nz)
            def _(k):
                ut[:, pl.ds(pl.multiple_of(k * block, block), block)] = uall[k].T

        remote(cb.at[it], cb.at[it], cb_s, cb_r.at[it], to_b(bid + 1)).wait_recv()
        total = ps[it]
        for k in range(1, nb):
            total = total + cb[it, k - 1]
        scale = 1.0 / total
        if it == 0:
            u_forward(u_first, 0)
        rowsum(scale)
        if it == ITERS - 1:
            cps = scale
        pay[it] = ccs[...].astype(BF16)
        for kx, kz in others:
            pb_copy(it, kx, kz).start()
        if it == 0:
            e_blocks([0])
        elif it == 1:
            e_blocks(u_second)
        else:
            pb_landed(ITERS)
            cinv[...] = 1.0 / pb_total(ITERS)
        pb_landed(it)
        ccs[...] = 1.0 / pb_total(it)


    drain.append(lambda: gone(u_s, (nx - 1) * nz + nz - 1))
    drain.append(lambda: remote(cb, cb, cb_s, cb_r.at[0], to_b(bid + 1)).wait_send())
    drain.append(lambda: remote(pb, pb, pb_s, pb_r.at[0], to_xz(x, z + 1)).wait_send())

    def fn_copy(d):
        i = near_z.index(d)
        return remote(
            ugb.at[(z + d) % nz], near.at[i], f_s, fn_r.at[i], to_xz(x, z + d)
        )

    def fx_copy(d, k):
        xx = (x + k) % nx
        return remote(
            ugb.at[(z + d) % nz, pl.ds(pl.multiple_of(xx * rows, rows), rows)],
            xr.at[k - 1, d], f_s, fx_r.at[d], to_xz(xx, z),
        )

    def fz_copy(d):
        return remote(zs.at[d], zr.at[d], f_s, fz_r, to_xz(x, z + d))

    late = far_z[::-1]
    series = near_z + late + [0]
    pairs = [series[i : i + 2] for i in range(0, nz, 2)]

    @pl.loop(0, len(pairs))
    def _(s):
        blks = [(z + pick(s, [p[i] for p in pairs])) % nz for i in range(2)]
        invs, scas = [
            [
                jnp.concatenate([to_col(ref[pl.ds(blk * per + i, 1), :]) for i in range(per)], axis=0)
                for blk in blks
            ]
            for ref in (cinv, ccs)
        ]
        acc = jnp.zeros((2 * block, depth), F32)
        for j in range(width // tile):
            cols = slice(j * tile, (j + 1) * tile)
            both = []
            for blk, inv, sca in zip(blks, invs, scas):
                at = pl.ds(pl.multiple_of(blk * block, block), block)
                prob = e[at, cols] * inv
                target = (m[at, cols] * sca) * cps[:, cols]
                gh = (prob - target).astype(BF16)
                g[at, cols] = gh
                both.append(gh)
            acc += jnp.dot(jnp.concatenate(both, axis=0), spt[cols, :], preferred_element_type=F32)
        for i, blk in enumerate(blks):
            ugb[blk] = acc[i * block : (i + 1) * block].astype(BF16)

        @pl.when(s == len(pairs) - 1)
        def _():
            ug0[...] = acc[block:]

        for i, p in enumerate(pairs):

            @pl.when(s == i)
            def _():
                for d in p:
                    if d in near_z:
                        fn_copy(d).start()
                    elif d:
                        for k in range(1, nx):
                            fx_copy(d, k).start()

    nch = width // chunk

    def pc_copy(j):
        cols = pl.ds(pl.multiple_of(j * chunk, chunk), chunk)
        return remote(
            pgb.at[1 - c, :, :, cols], cr.at[:, :, cols], p_s, pc_r.at[j], to_b(y * 2 + 1 - c)
        )

    def py_copy(j, k):
        cols = pl.ds(pl.multiple_of(j * chunk, chunk), chunk)
        return remote(
            ys.at[k - 1, :, cols], yr.at[k - 1, :, cols],
            p_s, py_r.at[j], to_b(bid + 2 * k),
        )

    def pc_sum(j):
        cols = pl.ds(pl.multiple_of(j * chunk, chunk), chunk)
        pc_copy(j).wait_recv()
        for k in range(1, ny):
            yy = (y + k) % ny
            ys[k - 1, :, cols] = (pgf[c, yy, :, cols] + cr[yy, :, cols].astype(F32)).astype(BF16)
            py_copy(j, k).start()
        pg_out[:, cols] = pgf[c, y, :, cols] + cr[y, :, cols].astype(F32)

    def x_sum(d):
        landed(fx_r.at[d], nx - 1)
        total = ugb[(z + d) % nz, pl.ds(my, rows), :].astype(F32) if d else ug0[pl.ds(my, rows), :]
        for k in range(1, nx):
            total = total + xr[k - 1, d].astype(F32)
        return total

    def z_send(d):
        zs[d] = x_sum(d).astype(BF16)
        fz_copy(d).start()

    def own_rows():
        total = ug0[...]
        for i, d in enumerate(near_z):
            fn_copy(d).wait_recv()
            total = total + near[i].astype(F32)
        ug0[...] = total
        ugb[z] = total.astype(BF16)
        for k in range(1, nx):
            fx_copy(0, k).start()

    after = {1: ["own"], 2: late[:2], 3: late[2:3]}
    after = {j: a for j, a in after.items() if j < nch}
    done = [d for a in after.values() for d in a]
    rest = (["own"] if "own" not in done else []) + [d for d in late if d not in done]

    def act(d):
        own_rows() if d == "own" else z_send(d)

    @pl.loop(0, nch)
    def _(j):
        cols = pl.ds(pl.multiple_of(j * chunk, chunk), chunk)
        part = jnp.dot(ut[...], g[:, cols], preferred_element_type=F32)
        for yy in range(ny):
            for cc in range(2):
                d0 = (yy * 2 + cc) * dr
                pgf[cc, yy, :, cols] = part[d0 : d0 + dr]
                pgb[cc, yy, :, cols] = part[d0 : d0 + dr].astype(BF16)
        pc_copy(j).start()

        @pl.when(j > 0)
        def _():
            pc_sum(j - 1)

        for jj, ds in after.items():

            @pl.when(j == jj)
            def _():
                for d in ds:
                    act(d)

    pc_sum(nch - 1)
    for d in rest:
        act(d)
    total = x_sum(0)
    landed(fz_r, len(late))
    for d in late:
        total = total + zr[d].astype(F32)
    total = total / STUDENT_TEMP
    unit, norm = unit_rows(sf[...])
    inner = jnp.sum(unit * total, axis=1, keepdims=True)
    fg_out[...] = (total - unit * inner) / norm

    @pl.loop(0, nch)
    def _(j):
        cols = pl.ds(pl.multiple_of(j * chunk, chunk), chunk)
        total = pg_out[:, cols]
        landed(py_r.at[j], (ny - 1) * dr * chunk * 2 // row_bytes)
        for k in range(1, ny):
            total = total + yr[k - 1, :, cols].astype(F32)
        pg_out[:, cols] = total / STUDENT_TEMP

    drain.append(lambda: gone(f_s, nx * len(near_z) + (nx - 1) * (len(late) + 1) + len(late)))
    drain.append(lambda: gone(p_s, (2 * ny - 1) * dr * width * 2 // row_bytes))
    for leave in drain:
        leave()


def shards(nx, nz, ny, student_feats, teacher_feats, student_protos, teacher_protos):
    rows, depth = student_feats.shape
    width = student_protos.shape[1]
    block, nb = nx * rows, 2 * ny
    crops, dr = nz * block, depth // nb
    groups = crops // LANES
    chunk = min(512, width)
    nch = width // chunk
    one = lambda n: max(n, 1)
    x1, y1, b1 = one(nx - 1), one(ny - 1), nb - 1
    dma = pltpu.SemaphoreType.DMA
    vmem = pl.BlockSpec(memory_space=pltpu.VMEM)
    hbm = pl.BlockSpec(memory_space=pl.ANY)
    scratch = [
        pltpu.VMEM((depth, width), BF16),
        pltpu.VMEM((depth, width), BF16),
        pltpu.VMEM((width, depth), BF16),
        pltpu.VMEM((nz, block, depth), BF16),
        pltpu.VMEM((nz, block, depth), BF16),
        pltpu.VMEM((depth, crops), BF16),
        pltpu.VMEM((crops, width), F32),
        pltpu.VMEM((crops, width), F32),
        pltpu.VMEM((crops, width), BF16),
        pltpu.VMEM((8, width), F32),
        pltpu.VMEM((ITERS, 1, width), F32),
        pltpu.VMEM((groups, LANES), F32),
        pltpu.VMEM((ITERS + 1, groups, LANES), BF16),
        pltpu.VMEM((groups, LANES), F32),
        pltpu.VMEM((groups, LANES), F32),
        pltpu.VMEM((ITERS, b1, 1, width), F32),
        pltpu.VMEM((ITERS + 1, nx * nz - 1, groups, LANES), BF16),
        pltpu.VMEM((nz, block, depth), BF16),
        pltpu.VMEM((block, depth), F32),
        pltpu.VMEM((2, block, depth), BF16),
        pltpu.VMEM((x1, nz, rows, depth), BF16),
        pltpu.VMEM((nz, rows, depth), BF16),
        pltpu.VMEM((nz, rows, depth), BF16),
        pltpu.VMEM((2, ny, dr, width), F32),
        pltpu.VMEM((2, ny, dr, width), BF16),
        pltpu.VMEM((ny, dr, width), BF16),
        pltpu.VMEM((y1, dr, width), BF16),
        pltpu.VMEM((y1, dr, width), BF16),
        dma((2,)),
        dma((nz,)), dma((nz,)), dma((2,)), dma((nz,)),
        dma((ITERS,)), dma((ITERS + 1,)), dma((2,)), dma((nz,)), dma, dma((nch,)), dma((nch,)),
        dma, dma, dma, dma, dma, dma,
        pltpu.VMEM((nx * nz, rows, depth), BF16),
    ]
    return pl.pallas_call(
        functools.partial(kernel, nx, nz, ny),
        out_shape=(
            jax.ShapeDtypeStruct((dr, width), F32),
            jax.ShapeDtypeStruct((rows, depth), F32),
        ),
        in_specs=[vmem, vmem, hbm, hbm],
        out_specs=(vmem, vmem),
        scratch_shapes=scratch,
        compiler_params=pltpu.CompilerParams(
            collective_id=0, has_side_effects=True, vmem_limit_bytes=60 * 1024 * 1024
        ),
        cost_estimate=pl.CostEstimate(
            flops=8 * crops * width * depth, bytes_accessed=4 * depth * width,
            transcendentals=2 * crops * width,
        ),
    )(student_feats, teacher_feats, student_protos, teacher_protos)


def solution(mesh, nz=8):
    nx, ny = mesh.shape["proto"] // nz, mesh.shape["batch"] // 2
    in_specs = (
        P(("batch", "proto"), None),
        P(("batch", "proto"), None),
        P(None, "proto"),
        P(None, "proto"),
    )
    out_specs = (P("batch", "proto"), P(("batch", "proto"), None))
    return jax.shard_map(
        functools.partial(shards, nx, nz, ny),
        mesh=mesh, in_specs=in_specs, out_specs=out_specs, check_vma=False,
    )
```

```python
import functools

import jax
import jax.numpy as jnp
from jax import lax
from jax.experimental import pallas as pl
from jax.experimental.pallas import tpu as pltpu
from jax.sharding import PartitionSpec as P

ITERS = 3
STUDENT_TEMP = 0.1
TEACHER_TEMP = 0.07
LOG2E = 1.4426950408889634
MESH = pl.DeviceIdType.MESH
F32 = jnp.float32
BF16 = jnp.bfloat16
LANES = 128


def unit_rows(feats):
    values = feats.astype(F32)
    norm = jnp.sqrt(jnp.sum(values * values, axis=1, keepdims=True) + 1e-06)
    return values / norm, norm


def kernel(
    nx, nz, ny,
    sf, tf, sp_hbm, tp_hbm,
    pg_out, fg_out,
    tp, sp, spt, tall, uall, ut, uts, m, e, g,
    colacc, ps, lse_acc, crop_acc, pay, cinv, ccs, own_col,
    cb, pb,
    ugb, ug0, near, xr, zs, zr,
    pgf, pgb, cr, ys, yr,
    local_s,
    tz_r, tx_r, uz_r, ux_r, cb_r, pb_r, fn_r, fx_r, fz_r, pc_r, py_r,
    t_s, u_s, cb_s, pb_s, f_s, p_s,
    spare,
):
    rows = sf.shape[0]
    depth, width = tp.shape
    block = nx * rows
    crops = nz * block
    nb = 2 * ny
    dr = depth // nb
    tile = min(256, width)
    groups = crops // LANES
    per = block // LANES
    chunk = min(512, width)

    pid = lax.axis_index("proto")
    bid = lax.axis_index("batch")
    x, z = pid // nz, pid % nz
    y, c = bid // 2, bid % 2
    my = pl.multiple_of(x * rows, rows)

    def to_xz(xx, zz):
        return {"proto": (xx % nx) * nz + zz % nz}

    def to_b(bb):
        return {"batch": bb % nb}

    def remote(src, dst, ss, rs, dev):
        return pltpu.make_async_remote_copy(
            src_ref=src, dst_ref=dst, send_sem=ss, recv_sem=rs, device_id=dev, device_id_type=MESH
        )

    drain = []

    row_bytes = rows * depth * 2

    def landed(sem, count):
        if count:
            ref = spare.at[pl.ds(0, count)]
            remote(ref, ref, sem, sem, to_xz(x, z + 1)).wait_recv()

    def gone(sem, count):
        if count:
            ref = spare.at[pl.ds(0, count)]
            remote(ref, ref, sem, sem, to_xz(x, z + 1)).wait_send()

    barrier = pltpu.get_barrier_semaphore()
    for k in range(1, nx):
        pl.semaphore_signal(barrier, inc=1, device_id=to_xz(x + k, z), device_id_type=MESH)
    for k in range(1, nz):
        pl.semaphore_signal(barrier, inc=1, device_id=to_xz(x, z + k), device_id_type=MESH)
    for k in range(1, nb):
        pl.semaphore_signal(barrier, inc=1, device_id=to_b(bid + k), device_id_type=MESH)

    load_tp = pltpu.make_async_copy(tp_hbm, tp, local_s.at[0])
    load_sp = pltpu.make_async_copy(sp_hbm, sp, local_s.at[1])
    load_tp.start()
    load_sp.start()

    tall[z, pl.ds(my, rows), :] = unit_rows(tf[...])[0].astype(BF16)
    uall[z, pl.ds(my, rows), :] = unit_rows(sf[...])[0].astype(BF16)
    colacc[...] = jnp.zeros_like(colacc)
    eye = lax.broadcasted_iota(jnp.int32, (LANES, LANES), 0) == lax.broadcasted_iota(
        jnp.int32, (LANES, LANES), 1
    )

    def to_row(col):
        return jnp.sum(jnp.where(eye, col, 0.0), axis=0, keepdims=True)

    def to_col(row):
        return jnp.sum(jnp.where(eye, row, 0.0), axis=1, keepdims=True)

    pl.semaphore_wait(barrier, (nx - 1) + (nz - 1) + (nb - 1))

    near_z = sorted({1, nz - 1})
    far_z = [d for d in range(1, nz) if d not in near_z]
    far_z = sorted(far_z, key=lambda d: (min(d, nz - d), d))

    u_order = [d for d in range(1, nz)]
    cut = (len(u_order) - 1) // 2
    u_first, u_second = u_order[:cut], u_order[cut:]

    def tz(d):
        ref = tall.at[z, pl.ds(my, rows)]
        return remote(ref, ref, t_s, tz_r.at[d], to_xz(x, z + d))

    def trow(d):
        ref = tall.at[z]
        return remote(ref, ref, t_s, tz_r.at[d], to_xz(x, z + d))

    def tx(d, k):
        ref = tall.at[(z + nz - d) % nz, pl.ds(my, rows)]
        return remote(ref, ref, t_s, tx_r.at[d], to_xz(x + k, z))

    def uz(d):
        ref = uall.at[z, pl.ds(my, rows)]
        return remote(ref, ref, u_s, uz_r.at[0 if d in u_first else 1], to_xz(x, z + d))

    def ux(d, k):
        ref = uall.at[(z + nz - d) % nz, pl.ds(my, rows)]
        return remote(ref, ref, u_s, ux_r.at[d], to_xz(x + k, z))

    for k in range(1, nx):
        tx(0, k).start()
    for d in far_z:
        tz(d).start()

    def compute_m(blk):
        row0 = pl.multiple_of(blk * block, block)
        a = tall[blk]
        for j in range(width // tile):
            cols = slice(j * tile, (j + 1) * tile)
            s = jnp.dot(a, tp[:, cols], preferred_element_type=F32)
            v = jnp.exp2(s * (LOG2E / TEACHER_TEMP))
            m[pl.ds(row0, block), cols] = v
            colacc[:, cols] += jnp.sum(v.reshape(block // 8, 8, tile), axis=0)

    landed(tx_r.at[0], nx - 1)
    for d in near_z:
        trow(d).start()
    load_tp.wait()
    compute_m(z)
    for d in far_z:
        tz(d).wait_recv()
        for k in range(1, nx):
            tx(d, k).start()
    for k in range(1, nx):
        ux(0, k).start()
    for d in range(1, nz):
        uz(d).start()

    def pick(s, table):
        out = jnp.int32(table[0])
        for i in range(1, len(table)):
            out = jnp.where(s == i, table[i], out)
        return out

    arrivals = far_z[:2] + near_z + far_z[2:]

    @pl.loop(0, nz - 1)
    def _(s):
        d = pick(s, arrivals)
        is_near = (d == 1) | (d == nz - 1)

        @pl.when(is_near)
        def _():
            trow(d).wait_recv()

        @pl.when(jnp.logical_not(is_near))
        def _():
            landed(tx_r.at[d], nx - 1)

        compute_m((z + nz - d) % nz)

    drain.append(lambda: gone(t_s, (nx - 1) * (1 + len(far_z)) + len(far_z) + nx * len(near_z)))

    def cb_copy(it, k):
        return remote(
            ps.at[it], cb.at[it, k - 1], cb_s, cb_r.at[it], to_b(bid + k)
        )

    def pb_copy(it, kx, kz):
        i = kx * nz + kz - 1
        return remote(
            pay.at[it], pb.at[it, i], pb_s, pb_r.at[it], to_xz(x + kx, z + kz)
        )

    others = [(kx, kz) for kx in range(nx) for kz in range(nz) if kx or kz]

    def pb_landed(it):
        remote(pb.at[it], pb.at[it], pb_s, pb_r.at[it], to_xz(x, z + 1)).wait_recv()

    def pb_total(it):
        total = pay[it].astype(F32)
        for i in range(nx * nz - 1):
            total = total + pb[it, i].astype(F32)
        return total

    def compute_e(blk):
        row0 = pl.multiple_of(blk * block, block)
        a = uall[blk]
        ut[:, pl.ds(row0, block)] = a.T
        acc = jnp.zeros((block, LANES), F32)
        grad = jnp.zeros((block, depth), F32)
        for j in range(width // tile):
            cols = slice(j * tile, (j + 1) * tile)
            s = jnp.dot(a, sp[:, cols], preferred_element_type=F32)
            v = jnp.exp2(jnp.minimum(s * (LOG2E / STUDENT_TEMP), 128.0) - 18.0)
            half = v.astype(BF16)
            e[pl.ds(row0, block), cols] = half
            for t in range(tile // LANES):
                acc += v[:, t * LANES : (t + 1) * LANES]
            grad += jnp.dot(half, spt[cols, :], preferred_element_type=F32)
        ugb[0, blk] = grad.astype(BF16)
        for i in range(per):
            col = jnp.sum(acc[i * LANES : (i + 1) * LANES], axis=1, keepdims=True)
            lse_acc[pl.ds(blk * per + i, 1), :] = to_row(col)
        return grad

    def e_blocks(ds):
        @pl.loop(0, len(ds))
        def _(s):
            d = pick(s, ds)
            landed(ux_r.at[d], nx - 1)
            compute_e((z + nz - d) % nz)

    def u_forward(ds, i):
        landed(uz_r.at[i], len(ds))
        for d in ds:
            for k in range(1, nx):
                ux(d, k).start()

    def colsum():
        def body(i, acc):
            col = to_col(ccs[pl.ds(i, 1), :])
            for q in range(LANES // 8):
                acc = acc + m[pl.ds(i * LANES + q * 8, 8), :] * col[q * 8 : (q + 1) * 8]
            return acc

        return lax.fori_loop(0, groups, body, jnp.zeros((8, width), F32), unroll=min(4, groups))

    def rowsum(scale):
        def body(i):
            acc = jnp.zeros((LANES, LANES), F32)
            for t in range(width // LANES):
                cols = slice(t * LANES, (t + 1) * LANES)
                acc = acc + m[pl.ds(i * LANES, LANES), cols] * scale[:, cols]
            crop_acc[pl.ds(i, 1), :] = to_row(jnp.sum(acc, axis=1, keepdims=True))

        pl.loop(0, groups, unroll=min(4, groups))(body)

    late = far_z[::-1]
    nch = width // chunk

    def fn_copy(q, d):
        i = near_z.index(d)
        return remote(
            ugb.at[q, (z + d) % nz], near.at[q, i], f_s.at[q], fn_r.at[q, i], to_xz(x, z + d)
        )

    def fx_copy(q, d, k):
        xx = (x + k) % nx
        return remote(
            ugb.at[q, (z + d) % nz, pl.ds(pl.multiple_of(xx * rows, rows), rows)],
            xr.at[q, k - 1, d], f_s.at[q], fx_r.at[q, d], to_xz(xx, z),
        )

    def fz_copy(q, d):
        return remote(zs.at[q, d], zr.at[q, d], f_s.at[q], fz_r.at[q], to_xz(x, z + d))

    def x_sum(q, d):
        landed(fx_r.at[q, d], nx - 1)
        total = ugb[q, (z + d) % nz, pl.ds(my, rows), :].astype(F32) if d else ug0[q, pl.ds(my, rows), :]
        for k in range(1, nx):
            total = total + xr[q, k - 1, d].astype(F32)
        return total

    def z_send(q, d):
        zs[q, d] = x_sum(q, d).astype(BF16)
        fz_copy(q, d).start()

    def own_rows(q):
        total = ug0[q]
        for i, d in enumerate(near_z):
            fn_copy(q, d).wait_recv()
            total = total + near[q, i].astype(F32)
        ug0[q] = total
        ugb[q, z] = total.astype(BF16)
        for k in range(1, nx):
            fx_copy(q, 0, k).start()

    def f_send(q, d):
        if d in near_z:
            fn_copy(q, d).start()
        elif d:
            for k in range(1, nx):
                fx_copy(q, d, k).start()

    def f_total(q):
        total = x_sum(q, 0)
        landed(fz_r.at[q], len(late))
        for d in late:
            total = total + zr[q, d].astype(F32)
        return total

    series = near_z + late + [0]
    pairs = [series[i : i + 2] for i in range(0, nz, 2)]

    def targets(scale):
        @pl.loop(0, len(pairs))
        def _(s):
            blks = [(z + pick(s, [p[i] for p in pairs])) % nz for i in range(2)]
            scas = [
                jnp.concatenate([to_col(ccs[pl.ds(blk * per + i, 1), :]) for i in range(per)], axis=0)
                for blk in blks
            ]
            acc = jnp.zeros((2 * block, depth), F32)
            for j in range(width // tile):
                cols = slice(j * tile, (j + 1) * tile)
                both = []
                for blk, sca in zip(blks, scas):
                    at = pl.ds(pl.multiple_of(blk * block, block), block)
                    gh = ((m[at, cols] * sca) * scale[:, cols]).astype(BF16)
                    g[at, cols] = gh
                    both.append(gh)
                acc += jnp.dot(jnp.concatenate(both, axis=0), spt[cols, :], preferred_element_type=F32)
            for i, blk in enumerate(blks):
                ugb[1, blk] = acc[i * block : (i + 1) * block].astype(BF16)

            @pl.when(s == len(pairs) - 1)
            def _():
                ug0[1] = acc[block:]

            for i, p in enumerate(pairs):

                @pl.when(s == i)
                def _():
                    for d in p:
                        f_send(1, d)

    def scaled_ut(ref):
        def body(i):
            cols = pl.ds(pl.multiple_of(i * LANES, LANES), LANES)
            uts[:, cols] = (ut[:, cols].astype(F32) * ref[pl.ds(i, 1), :]).astype(BF16)

        pl.loop(0, groups, unroll=min(4, groups))(body)

    def probs_part():
        scaled_ut(cinv)

        @pl.loop(0, nch)
        def _(j):
            cols = pl.ds(pl.multiple_of(j * chunk, chunk), chunk)
            part = jnp.dot(uts[...], e[:, cols], preferred_element_type=F32)
            for yy in range(ny):
                for cc in range(2):
                    d0 = (yy * 2 + cc) * dr
                    pgf[cc, yy, :, cols] = part[d0 : d0 + dr]

    for it in range(ITERS):
        part = colacc[...] if it == 0 else colsum()
        ps[it] = jnp.sum(part, axis=0, keepdims=True)
        for k in range(1, nb):
            cb_copy(it, k).start()
        if it == 0:
            load_sp.wait()

            @pl.loop(0, width // tile)
            def _(j):
                cols = pl.ds(pl.multiple_of(j * tile, tile), tile)
                spt[cols, :] = sp[:, cols].T

        elif it == 1:
            u_forward(u_second, 1)
            e_blocks(u_first)
        else:
            pay[ITERS] = lse_acc[...].astype(BF16)
            for kx, kz in others:
                pb_copy(ITERS, kx, kz).start()
            for d in u_second:
                f_send(0, nz - d)

        remote(cb.at[it], cb.at[it], cb_s, cb_r.at[it], to_b(bid + 1)).wait_recv()
        total = ps[it]
        for k in range(1, nb):
            total = total + cb[it, k - 1]
        scale = 1.0 / total
        if it == 0:
            u_forward(u_first, 0)
        rowsum(scale)
        pay[it] = crop_acc[...].astype(BF16)
        for kx, kz in others:
            pb_copy(it, kx, kz).start()
        if it == 0:
            landed(ux_r.at[0], nx - 1)
            ug0[0] = compute_e(z)
        elif it == 1:
            for d in u_first:
                f_send(0, nz - d)
            e_blocks(u_second)
        else:
            targets(scale)
            pb_landed(ITERS)
            cinv[...] = 1.0 / pb_total(ITERS)
            own_rows(0)
            for d in late:
                z_send(0, d)
            probs_part()
        pb_landed(it)
        if it < ITERS - 1:
            ccs[...] = 1.0 / pb_total(it)
        else:
            ccs[...] = 1.0 / (pb_total(it) * ccs[...])


    drain.append(lambda: gone(u_s, (nx - 1) * nz + nz - 1))
    drain.append(lambda: remote(cb, cb, cb_s, cb_r.at[0], to_b(bid + 1)).wait_send())
    drain.append(lambda: remote(pb, pb, pb_s, pb_r.at[0], to_xz(x, z + 1)).wait_send())

    def pc_copy(j):
        cols = pl.ds(pl.multiple_of(j * chunk, chunk), chunk)
        return remote(
            pgb.at[1 - c, :, :, cols], cr.at[:, :, cols], p_s, pc_r.at[j], to_b(y * 2 + 1 - c)
        )

    def py_copy(j, k):
        cols = pl.ds(pl.multiple_of(j * chunk, chunk), chunk)
        return remote(
            ys.at[k - 1, :, cols], yr.at[k - 1, :, cols],
            p_s, py_r.at[j], to_b(bid + 2 * k),
        )

    def pc_sum(j):
        cols = pl.ds(pl.multiple_of(j * chunk, chunk), chunk)
        pc_copy(j).wait_recv()
        for k in range(1, ny):
            yy = (y + k) % ny
            ys[k - 1, :, cols] = (pgf[c, yy, :, cols] + cr[yy, :, cols].astype(F32)).astype(BF16)
            py_copy(j, k).start()
        pg_out[:, cols] = pgf[c, y, :, cols] + cr[y, :, cols].astype(F32)

    scaled_ut(ccs)

    after = {0: ["own"] + late[:1], 1: late[1:2], 2: late[2:4]}
    after = {j: a for j, a in after.items() if j < nch}
    done = [d for a in after.values() for d in a]
    rest = (["own"] if "own" not in done else []) + [d for d in late if d not in done]

    def act(d):
        own_rows(1) if d == "own" else z_send(1, d)

    @pl.loop(0, nch)
    def _(j):
        cols = pl.ds(pl.multiple_of(j * chunk, chunk), chunk)
        part = jnp.dot(uts[...], g[:, cols], preferred_element_type=F32)
        for yy in range(ny):
            for cc in range(2):
                d0 = (yy * 2 + cc) * dr
                diff = pgf[cc, yy, :, cols] - part[d0 : d0 + dr]
                pgf[cc, yy, :, cols] = diff
                pgb[cc, yy, :, cols] = diff.astype(BF16)
        pc_copy(j).start()

        @pl.when(j > 0)
        def _():
            pc_sum(j - 1)

        for jj, ds in after.items():

            @pl.when(j == jj)
            def _():
                for d in ds:
                    act(d)

    pc_sum(nch - 1)
    for d in rest:
        act(d)
    part = z * per + my // LANES
    for q, ref in enumerate((cinv, ccs)):
        own_col[q] = jnp.broadcast_to(to_col(ref[pl.ds(part, 1), :]), (LANES, LANES))
    low = pl.multiple_of(my % LANES, min(rows, LANES))
    inv, rho = [own_col[q, pl.ds(low, rows), 0:1] for q in range(2)]
    total = f_total(0) * inv - f_total(1) * rho
    total = total / STUDENT_TEMP
    unit, norm = unit_rows(sf[...])
    inner = jnp.sum(unit * total, axis=1, keepdims=True)
    fg_out[...] = (total - unit * inner) / norm

    @pl.loop(0, nch)
    def _(j):
        cols = pl.ds(pl.multiple_of(j * chunk, chunk), chunk)
        total = pg_out[:, cols]
        landed(py_r.at[j], (ny - 1) * dr * chunk * 2 // row_bytes)
        for k in range(1, ny):
            total = total + yr[k - 1, :, cols].astype(F32)
        pg_out[:, cols] = total / STUDENT_TEMP

    drain.append(lambda: gone(f_s.at[0], nx * len(near_z) + (nx - 1) * (len(late) + 1) + len(late)))
    drain.append(lambda: gone(f_s.at[1], nx * len(near_z) + (nx - 1) * (len(late) + 1) + len(late)))
    drain.append(lambda: gone(p_s, (2 * ny - 1) * dr * width * 2 // row_bytes))
    for leave in drain:
        leave()


def shards(nx, nz, ny, student_feats, teacher_feats, student_protos, teacher_protos):
    rows, depth = student_feats.shape
    width = student_protos.shape[1]
    block, nb = nx * rows, 2 * ny
    crops, dr = nz * block, depth // nb
    groups = crops // LANES
    chunk = min(512, width)
    nch = width // chunk
    one = lambda n: max(n, 1)
    x1, y1, b1 = one(nx - 1), one(ny - 1), nb - 1
    dma = pltpu.SemaphoreType.DMA
    vmem = pl.BlockSpec(memory_space=pltpu.VMEM)
    hbm = pl.BlockSpec(memory_space=pl.ANY)
    scratch = [
        pltpu.VMEM((depth, width), BF16),
        pltpu.VMEM((depth, width), BF16),
        pltpu.VMEM((width, depth), BF16),
        pltpu.VMEM((nz, block, depth), BF16),
        pltpu.VMEM((nz, block, depth), BF16),
        pltpu.VMEM((depth, crops), BF16),
        pltpu.VMEM((depth, crops), BF16),
        pltpu.VMEM((crops, width), F32),
        pltpu.VMEM((crops, width), BF16),
        pltpu.VMEM((crops, width), BF16),
        pltpu.VMEM((8, width), F32),
        pltpu.VMEM((ITERS, 1, width), F32),
        pltpu.VMEM((groups, LANES), F32),
        pltpu.VMEM((groups, LANES), F32),
        pltpu.VMEM((ITERS + 1, groups, LANES), BF16),
        pltpu.VMEM((groups, LANES), F32),
        pltpu.VMEM((groups, LANES), F32),
        pltpu.VMEM((2, LANES, LANES), F32),
        pltpu.VMEM((ITERS, b1, 1, width), F32),
        pltpu.VMEM((ITERS + 1, nx * nz - 1, groups, LANES), BF16),
        pltpu.VMEM((2, nz, block, depth), BF16),
        pltpu.VMEM((2, block, depth), F32),
        pltpu.VMEM((2, 2, block, depth), BF16),
        pltpu.VMEM((2, x1, nz, rows, depth), BF16),
        pltpu.VMEM((2, nz, rows, depth), BF16),
        pltpu.VMEM((2, nz, rows, depth), BF16),
        pltpu.VMEM((2, ny, dr, width), F32),
        pltpu.VMEM((2, ny, dr, width), BF16),
        pltpu.VMEM((ny, dr, width), BF16),
        pltpu.VMEM((y1, dr, width), BF16),
        pltpu.VMEM((y1, dr, width), BF16),
        dma((2,)),
        dma((nz,)), dma((nz,)), dma((2,)), dma((nz,)),
        dma((ITERS,)), dma((ITERS + 1,)), dma((2, 2)), dma((2, nz)), dma((2,)), dma((nch,)), dma((nch,)),
        dma, dma, dma, dma, dma((2,)), dma,
        pltpu.VMEM((nx * nz, rows, depth), BF16),
    ]
    return pl.pallas_call(
        functools.partial(kernel, nx, nz, ny),
        out_shape=(
            jax.ShapeDtypeStruct((dr, width), F32),
            jax.ShapeDtypeStruct((rows, depth), F32),
        ),
        in_specs=[vmem, vmem, hbm, hbm],
        out_specs=(vmem, vmem),
        scratch_shapes=scratch,
        compiler_params=pltpu.CompilerParams(
            collective_id=0, has_side_effects=True, vmem_limit_bytes=60 * 1024 * 1024
        ),
        cost_estimate=pl.CostEstimate(
            flops=12 * crops * width * depth, bytes_accessed=4 * depth * width,
            transcendentals=2 * crops * width,
        ),
    )(student_feats, teacher_feats, student_protos, teacher_protos)


def solution(mesh, nz=8):
    nx, ny = mesh.shape["proto"] // nz, mesh.shape["batch"] // 2
    in_specs = (
        P(("batch", "proto"), None),
        P(("batch", "proto"), None),
        P(None, "proto"),
        P(None, "proto"),
    )
    out_specs = (P("batch", "proto"), P(("batch", "proto"), None))
    return jax.shard_map(
        functools.partial(shards, nx, nz, ny),
        mesh=mesh, in_specs=in_specs, out_specs=out_specs, check_vma=False,
    )
```

```python
import functools

import jax
import jax.numpy as jnp
from jax import lax
from jax.experimental import pallas as pl
from jax.experimental.pallas import tpu as pltpu
from jax.sharding import PartitionSpec as P

ITERS = 3
STUDENT_TEMP = 0.1
TEACHER_TEMP = 0.07
LOG2E = 1.4426950408889634
MESH = pl.DeviceIdType.MESH
F32 = jnp.float32
BF16 = jnp.bfloat16
LANES = 128


def unit_rows(feats):
    values = feats.astype(F32)
    norm = jnp.sqrt(jnp.sum(values * values, axis=1, keepdims=True) + 1e-06)
    return values / norm, norm


def kernel(
    nx, nz, ny,
    sf, tf, sp_hbm, tp_hbm,
    pg_out, fg_out,
    tp, sp, spt, tall, uall, ut, uts, m, e, g,
    colacc, racc, ps, lse_acc, crop_acc, pay, pay_l, cinv, ccs, own_col,
    cb, pb, pbl,
    ugb, ug0, near, xr, zs, zr,
    pgf, pgb, cr, ys, yr,
    local_s,
    tz_r, tx_r, uz_r, ux_r, cb_r, pb_r, pbl_r, fn_r, fx_r, fz_r, pc_r, py_r,
    t_s, u_s, cb_s, pb_s, f_s, p_s,
    spare,
):
    rows = sf.shape[0]
    depth, width = tp.shape
    block = nx * rows
    crops = nz * block
    nb = 2 * ny
    dr = depth // nb
    tile = min(256, width)
    groups = crops // LANES
    per = block // LANES
    chunk = min(512, width)

    pid = lax.axis_index("proto")
    bid = lax.axis_index("batch")
    x, z = pid // nz, pid % nz
    y, c = bid // 2, bid % 2
    my = pl.multiple_of(x * rows, rows)

    def to_xz(xx, zz):
        return {"proto": (xx % nx) * nz + zz % nz}

    def to_b(bb):
        return {"batch": bb % nb}

    def remote(src, dst, ss, rs, dev):
        return pltpu.make_async_remote_copy(
            src_ref=src, dst_ref=dst, send_sem=ss, recv_sem=rs, device_id=dev, device_id_type=MESH
        )

    drain = []

    row_bytes = rows * depth * 2

    def landed(sem, count):
        if count:
            ref = spare.at[pl.ds(0, count)]
            remote(ref, ref, sem, sem, to_xz(x, z + 1)).wait_recv()

    def gone(sem, count):
        if count:
            ref = spare.at[pl.ds(0, count)]
            remote(ref, ref, sem, sem, to_xz(x, z + 1)).wait_send()

    barrier = pltpu.get_barrier_semaphore()
    for k in range(1, nx):
        pl.semaphore_signal(barrier, inc=1, device_id=to_xz(x + k, z), device_id_type=MESH)
    for k in range(1, nz):
        pl.semaphore_signal(barrier, inc=1, device_id=to_xz(x, z + k), device_id_type=MESH)
    for k in range(1, nb):
        pl.semaphore_signal(barrier, inc=1, device_id=to_b(bid + k), device_id_type=MESH)

    load_tp = pltpu.make_async_copy(tp_hbm, tp, local_s.at[0])
    load_sp = pltpu.make_async_copy(sp_hbm, sp, local_s.at[1])
    load_tp.start()
    load_sp.start()

    tall[z, pl.ds(my, rows), :] = unit_rows(tf[...])[0].astype(BF16)
    uall[z, pl.ds(my, rows), :] = unit_rows(sf[...])[0].astype(BF16)
    colacc[...] = jnp.zeros_like(colacc)
    eye = lax.broadcasted_iota(jnp.int32, (LANES, LANES), 0) == lax.broadcasted_iota(
        jnp.int32, (LANES, LANES), 1
    )

    def to_row(col):
        return jnp.sum(jnp.where(eye, col, 0.0), axis=0, keepdims=True)

    def to_col(row):
        return jnp.sum(jnp.where(eye, row, 0.0), axis=1, keepdims=True)

    pl.semaphore_wait(barrier, (nx - 1) + (nz - 1) + (nb - 1))

    near_z = sorted({1, nz - 1})
    far_z = [d for d in range(1, nz) if d not in near_z]
    far_z = sorted(far_z, key=lambda d: (min(d, nz - d), d))

    u_order = [d for d in range(1, nz)]
    cut = (len(u_order) - 1) // 2
    u_first, u_second = u_order[:cut], u_order[cut:]

    def tz(d):
        ref = tall.at[z, pl.ds(my, rows)]
        return remote(ref, ref, t_s, tz_r.at[d], to_xz(x, z + d))

    def trow(d):
        ref = tall.at[z]
        return remote(ref, ref, t_s, tz_r.at[d], to_xz(x, z + d))

    def tx(d, k):
        ref = tall.at[(z + nz - d) % nz, pl.ds(my, rows)]
        return remote(ref, ref, t_s, tx_r.at[d], to_xz(x + k, z))

    def uz(d):
        ref = uall.at[z, pl.ds(my, rows)]
        return remote(ref, ref, u_s, uz_r.at[0 if d in u_first else 1], to_xz(x, z + d))

    def ux(d, k):
        ref = uall.at[(z + nz - d) % nz, pl.ds(my, rows)]
        return remote(ref, ref, u_s, ux_r.at[d], to_xz(x + k, z))

    for k in range(1, nx):
        tx(0, k).start()
    for d in far_z:
        tz(d).start()

    def compute_m(blk):
        row0 = pl.multiple_of(blk * block, block)
        a = tall[blk]
        for j in range(width // tile):
            cols = slice(j * tile, (j + 1) * tile)
            s = jnp.dot(a, tp[:, cols], preferred_element_type=F32)
            v = jnp.exp2(s * (LOG2E / TEACHER_TEMP))
            m[pl.ds(row0, block), cols] = v
            colacc[:, cols] += jnp.sum(v.reshape(block // 8, 8, tile), axis=0)

    landed(tx_r.at[0], nx - 1)
    for d in near_z:
        trow(d).start()
    load_tp.wait()
    compute_m(z)
    for d in far_z:
        tz(d).wait_recv()
        for k in range(1, nx):
            tx(d, k).start()
    for k in range(1, nx):
        ux(0, k).start()
    for d in range(1, nz):
        uz(d).start()

    def pick(s, table):
        out = jnp.int32(table[0])
        for i in range(1, len(table)):
            out = jnp.where(s == i, table[i], out)
        return out

    arrivals = far_z[:2] + near_z + far_z[2:]

    @pl.loop(0, nz - 1)
    def _(s):
        d = pick(s, arrivals)
        is_near = (d == 1) | (d == nz - 1)

        @pl.when(is_near)
        def _():
            trow(d).wait_recv()

        @pl.when(jnp.logical_not(is_near))
        def _():
            landed(tx_r.at[d], nx - 1)

        compute_m((z + nz - d) % nz)

    drain.append(lambda: gone(t_s, (nx - 1) * (1 + len(far_z)) + len(far_z) + nx * len(near_z)))

    def cb_copy(it, h, k):
        return remote(
            ps.at[it, h], cb.at[it, h, k - 1], cb_s, cb_r.at[it, h], to_b(bid + k)
        )

    def pb_copy(it, h, kx, kz):
        i = kx * nz + kz - 1
        return remote(
            pay.at[it, h], pb.at[it, h, i], pb_s, pb_r.at[it, h], to_xz(x + kx, z + kz)
        )

    def pbl_copy(kx, kz):
        i = kx * nz + kz - 1
        return remote(pay_l, pbl.at[i], pb_s, pbl_r, to_xz(x + kx, z + kz))

    others = [(kx, kz) for kx in range(nx) for kz in range(nz) if kx or kz]

    def pb_total(it, h):
        remote(pb.at[it, h], pb.at[it, h], pb_s, pb_r.at[it, h], to_xz(x, z + 1)).wait_recv()
        total = pay[it, h].astype(F32)
        for i in range(nx * nz - 1):
            total = total + pb[it, h, i].astype(F32)
        return total

    def pbl_total():
        remote(pbl, pbl, pb_s, pbl_r, to_xz(x, z + 1)).wait_recv()
        total = pay_l[...].astype(F32)
        for i in range(nx * nz - 1):
            total = total + pbl[i].astype(F32)
        return total

    def compute_e(blk):
        row0 = pl.multiple_of(blk * block, block)
        a = uall[blk]
        ut[:, pl.ds(row0, block)] = a.T
        acc = jnp.zeros((block, LANES), F32)
        grad = jnp.zeros((block, depth), F32)
        for j in range(width // tile):
            cols = slice(j * tile, (j + 1) * tile)
            s = jnp.dot(a, sp[:, cols], preferred_element_type=F32)
            v = jnp.exp2(jnp.minimum(s * (LOG2E / STUDENT_TEMP), 128.0) - 18.0)
            half = v.astype(BF16)
            e[pl.ds(row0, block), cols] = half
            for t in range(tile // LANES):
                acc += v[:, t * LANES : (t + 1) * LANES]
            grad += jnp.dot(half, spt[cols, :], preferred_element_type=F32)
        ugb[0, blk] = grad.astype(BF16)
        for i in range(per):
            col = jnp.sum(acc[i * LANES : (i + 1) * LANES], axis=1, keepdims=True)
            lse_acc[pl.ds(blk * per + i, 1), :] = to_row(col)
        return grad

    def e_blocks(ds):
        @pl.loop(0, len(ds))
        def _(s):
            d = pick(s, ds)
            landed(ux_r.at[d], nx - 1)
            compute_e((z + nz - d) % nz)

    def u_forward(ds, i):
        landed(uz_r.at[i], len(ds))
        for d in ds:
            for k in range(1, nx):
                ux(d, k).start()

    hw, hg = width // 2, groups // 2

    def crop_col(i, keep):
        at = pl.ds(pl.multiple_of(i * LANES, LANES), LANES)
        if keep is None:
            return racc[at, :]
        col = jnp.broadcast_to(to_col(ccs[pl.ds(i, 1), :]), (LANES, LANES))
        if keep:
            racc[at, :] = col
        return col

    def colsum(h, lo, n, keep):
        def body(j, acc):
            i = h * hg + j
            col = crop_col(i, keep)
            for q in range(LANES // 8):
                part = m[pl.ds(pl.multiple_of(i * LANES + q * 8, 8), 8), lo : lo + n]
                acc = acc + part * col[q * 8 : (q + 1) * 8, 0:1]
            return acc

        return lax.fori_loop(0, hg, body, jnp.zeros((8, n), F32), unroll=min(4, hg))

    def rowsum_first(scale):
        def body(i):
            at = pl.ds(pl.multiple_of(i * LANES, LANES), LANES)
            acc = jnp.zeros((LANES, LANES), F32)
            for t in range(hw // LANES):
                cols = slice(t * LANES, (t + 1) * LANES)
                acc = acc + m[at, cols] * scale[:, cols]
            racc[at, :] = acc

        pl.loop(0, groups, unroll=min(2, groups))(body)

    def rowsum_second(scale, h):
        def body(j):
            i = h * hg + j
            at = pl.ds(pl.multiple_of(i * LANES, LANES), LANES)
            acc = racc[at, :]
            for t in range(hw // LANES):
                cols = slice(t * LANES, (t + 1) * LANES)
                acc = acc + m[at, hw + t * LANES : hw + (t + 1) * LANES] * scale[:, cols]
            crop_acc[pl.ds(i, 1), :] = to_row(jnp.sum(acc, axis=1, keepdims=True))

        pl.loop(0, hg, unroll=min(4, hg))(body)

    late = far_z[::-1]
    nch = width // chunk

    def fn_copy(q, d):
        i = near_z.index(d)
        return remote(
            ugb.at[q, (z + d) % nz], near.at[q, i], f_s.at[q], fn_r.at[q, i], to_xz(x, z + d)
        )

    def fx_copy(q, d, k):
        xx = (x + k) % nx
        return remote(
            ugb.at[q, (z + d) % nz, pl.ds(pl.multiple_of(xx * rows, rows), rows)],
            xr.at[q, k - 1, d], f_s.at[q], fx_r.at[q, d], to_xz(xx, z),
        )

    def fz_copy(q, d):
        return remote(zs.at[q, d], zr.at[q, d], f_s.at[q], fz_r.at[q], to_xz(x, z + d))

    def x_sum(q, d):
        landed(fx_r.at[q, d], nx - 1)
        total = ugb[q, (z + d) % nz, pl.ds(my, rows), :].astype(F32) if d else ug0[q, pl.ds(my, rows), :]
        for k in range(1, nx):
            total = total + xr[q, k - 1, d].astype(F32)
        return total

    def z_send(q, d):
        zs[q, d] = x_sum(q, d).astype(BF16)
        fz_copy(q, d).start()

    def own_rows(q):
        total = ug0[q]
        for i, d in enumerate(near_z):
            fn_copy(q, d).wait_recv()
            total = total + near[q, i].astype(F32)
        ug0[q] = total
        ugb[q, z] = total.astype(BF16)
        for k in range(1, nx):
            fx_copy(q, 0, k).start()

    def f_send(q, d):
        if d in near_z:
            fn_copy(q, d).start()
        elif d:
            for k in range(1, nx):
                fx_copy(q, d, k).start()

    def f_total(q):
        total = x_sum(q, 0)
        landed(fz_r.at[q], len(late))
        for d in late:
            total = total + zr[q, d].astype(F32)
        return total

    series = near_z + late + [0]
    pairs = [series[i : i + 2] for i in range(0, nz, 2)]

    def targets(scale):
        @pl.loop(0, len(pairs))
        def _(s):
            blks = [(z + pick(s, [p[i] for p in pairs])) % nz for i in range(2)]
            scas = [
                jnp.concatenate([to_col(ccs[pl.ds(blk * per + i, 1), :]) for i in range(per)], axis=0)
                for blk in blks
            ]
            acc = jnp.zeros((2 * block, depth), F32)
            for j in range(width // tile):
                cols = slice(j * tile, (j + 1) * tile)
                both = []
                for blk, sca in zip(blks, scas):
                    at = pl.ds(pl.multiple_of(blk * block, block), block)
                    gh = ((m[at, cols] * sca) * scale[:, cols]).astype(BF16)
                    g[at, cols] = gh
                    both.append(gh)
                acc += jnp.dot(jnp.concatenate(both, axis=0), spt[cols, :], preferred_element_type=F32)
            for i, blk in enumerate(blks):
                ugb[1, blk] = acc[i * block : (i + 1) * block].astype(BF16)

            @pl.when(s == len(pairs) - 1)
            def _():
                ug0[1] = acc[block:]

            for i, p in enumerate(pairs):

                @pl.when(s == i)
                def _():
                    for d in p:
                        f_send(1, d)

    def scaled_ut(ref):
        def body(i):
            cols = pl.ds(pl.multiple_of(i * LANES, LANES), LANES)
            uts[:, cols] = (ut[:, cols].astype(F32) * ref[pl.ds(i, 1), :]).astype(BF16)

        pl.loop(0, groups, unroll=min(4, groups))(body)

    def probs_part():
        scaled_ut(cinv)

        @pl.loop(0, nch)
        def _(j):
            cols = pl.ds(pl.multiple_of(j * chunk, chunk), chunk)
            part = jnp.dot(uts[...], e[:, cols], preferred_element_type=F32)
            for yy in range(ny):
                for cc in range(2):
                    d0 = (yy * 2 + cc) * dr
                    pgf[cc, yy, :, cols] = part[d0 : d0 + dr]

    def send_ps(it, h, part):
        ps[it, h] = jnp.sum(part, axis=0, keepdims=True)
        for k in range(1, nb):
            cb_copy(it, h, k).start()

    def proto_scale(it, h):
        remote(cb.at[it, h], cb.at[it, h], cb_s, cb_r.at[it, h], to_b(bid + 1)).wait_recv()
        total = ps[it, h]
        for k in range(1, nb):
            total = total + cb[it, h, k - 1]
        return 1.0 / total

    def crop_half(h):
        return pl.ds(h * hg, hg)

    for it in range(ITERS):
        if it == 0:
            for h in range(2):
                send_ps(it, h, colacc[:, h * hw : (h + 1) * hw])
        else:
            ccs[crop_half(0), :] = 1.0 / pb_total(it - 1, 0)
            colacc[...] = colsum(0, 0, width, False)
            ccs[crop_half(1), :] = 1.0 / pb_total(it - 1, 1)
            for h in range(2):
                send_ps(it, h, colacc[:, h * hw : (h + 1) * hw] + colsum(1, h * hw, hw, None if h else True))
        if it == 0:
            load_sp.wait()

            @pl.loop(0, width // tile)
            def _(j):
                cols = pl.ds(pl.multiple_of(j * tile, tile), tile)
                spt[cols, :] = sp[:, cols].T

        elif it == 1:
            u_forward(u_second, 1)
            e_blocks(u_first)
        else:
            pay_l[...] = lse_acc[...].astype(BF16)
            for kx, kz in others:
                pbl_copy(kx, kz).start()
            for d in u_second:
                f_send(0, nz - d)
        scales = [proto_scale(it, 0)]
        if it == 0:
            u_forward(u_first, 0)
        rowsum_first(scales[0])
        scales.append(proto_scale(it, 1))
        for h in range(2):
            rowsum_second(scales[1], h)
            pay[it, h] = crop_acc[crop_half(h), :].astype(BF16)
            for kx, kz in others:
                pb_copy(it, h, kx, kz).start()
        if it == 0:
            landed(ux_r.at[0], nx - 1)
            ug0[0] = compute_e(z)
        elif it == 1:
            for d in u_first:
                f_send(0, nz - d)
            e_blocks(u_second)
        else:
            targets(jnp.concatenate(scales, axis=1))
            cinv[...] = 1.0 / pbl_total()
            own_rows(0)
            for d in late:
                z_send(0, d)
            probs_part()
    for h in range(2):
        ccs[crop_half(h), :] = 1.0 / (pb_total(ITERS - 1, h) * ccs[crop_half(h), :])

    drain.append(lambda: gone(u_s, (nx - 1) * nz + nz - 1))
    drain.append(lambda: remote(cb, cb, cb_s, cb_r.at[0, 0], to_b(bid + 1)).wait_send())
    drain.append(lambda: remote(pb, pb, pb_s, pb_r.at[0, 0], to_xz(x, z + 1)).wait_send())
    drain.append(lambda: remote(pbl, pbl, pb_s, pbl_r, to_xz(x, z + 1)).wait_send())

    def pc_copy(j):
        cols = pl.ds(pl.multiple_of(j * chunk, chunk), chunk)
        return remote(
            pgb.at[1 - c, :, :, cols], cr.at[:, :, cols], p_s, pc_r.at[j], to_b(y * 2 + 1 - c)
        )

    def py_copy(j, k):
        cols = pl.ds(pl.multiple_of(j * chunk, chunk), chunk)
        return remote(
            ys.at[k - 1, :, cols], yr.at[k - 1, :, cols],
            p_s, py_r.at[j], to_b(bid + 2 * k),
        )

    def pc_sum(j):
        cols = pl.ds(pl.multiple_of(j * chunk, chunk), chunk)
        pc_copy(j).wait_recv()
        for k in range(1, ny):
            yy = (y + k) % ny
            ys[k - 1, :, cols] = (pgf[c, yy, :, cols] + cr[yy, :, cols].astype(F32)).astype(BF16)
            py_copy(j, k).start()
        pg_out[:, cols] = pgf[c, y, :, cols] + cr[y, :, cols].astype(F32)

    scaled_ut(ccs)

    after = {0: ["own"] + late[:1], 1: late[1:2], 2: late[2:4]}
    after = {j: a for j, a in after.items() if j < nch}
    done = [d for a in after.values() for d in a]
    rest = (["own"] if "own" not in done else []) + [d for d in late if d not in done]

    def act(d):
        own_rows(1) if d == "own" else z_send(1, d)

    @pl.loop(0, nch)
    def _(j):
        cols = pl.ds(pl.multiple_of(j * chunk, chunk), chunk)
        part = jnp.dot(uts[...], g[:, cols], preferred_element_type=F32)
        for yy in range(ny):
            for cc in range(2):
                d0 = (yy * 2 + cc) * dr
                diff = pgf[cc, yy, :, cols] - part[d0 : d0 + dr]
                pgf[cc, yy, :, cols] = diff
                pgb[cc, yy, :, cols] = diff.astype(BF16)
        pc_copy(j).start()

        @pl.when(j > 0)
        def _():
            pc_sum(j - 1)

        for jj, ds in after.items():

            @pl.when(j == jj)
            def _():
                for d in ds:
                    act(d)

    pc_sum(nch - 1)
    for d in rest:
        act(d)
    part = z * per + my // LANES
    for q, ref in enumerate((cinv, ccs)):
        own_col[q] = jnp.broadcast_to(to_col(ref[pl.ds(part, 1), :]), (LANES, LANES))
    low = pl.multiple_of(my % LANES, min(rows, LANES))
    inv, rho = [own_col[q, pl.ds(low, rows), 0:1] for q in range(2)]
    total = f_total(0) * inv - f_total(1) * rho
    unit, norm = unit_rows(sf[...])
    inner = jnp.sum(unit * total, axis=1, keepdims=True)
    fg_out[...] = (total - unit * inner) / norm

    @pl.loop(0, nch)
    def _(j):
        cols = pl.ds(pl.multiple_of(j * chunk, chunk), chunk)
        total = pg_out[:, cols]
        landed(py_r.at[j], (ny - 1) * dr * chunk * 2 // row_bytes)
        for k in range(1, ny):
            total = total + yr[k - 1, :, cols].astype(F32)
        pg_out[:, cols] = total

    drain.append(lambda: gone(f_s.at[0], nx * len(near_z) + (nx - 1) * (len(late) + 1) + len(late)))
    drain.append(lambda: gone(f_s.at[1], nx * len(near_z) + (nx - 1) * (len(late) + 1) + len(late)))
    drain.append(lambda: gone(p_s, (2 * ny - 1) * dr * width * 2 // row_bytes))
    for leave in drain:
        leave()


def scale_out(a, b, a_out, b_out):
    a_out[...] = a[...] / STUDENT_TEMP
    b_out[...] = b[...] / STUDENT_TEMP


def shards(nx, nz, ny, student_feats, teacher_feats, student_protos, teacher_protos):
    rows, depth = student_feats.shape
    width = student_protos.shape[1]
    block, nb = nx * rows, 2 * ny
    crops, dr = nz * block, depth // nb
    groups = crops // LANES
    chunk = min(512, width)
    nch = width // chunk
    one = lambda n: max(n, 1)
    x1, y1, b1 = one(nx - 1), one(ny - 1), nb - 1
    dma = pltpu.SemaphoreType.DMA
    vmem = pl.BlockSpec(memory_space=pltpu.VMEM)
    hbm = pl.BlockSpec(memory_space=pl.ANY)
    scratch = [
        pltpu.VMEM((depth, width), BF16),
        pltpu.VMEM((depth, width), BF16),
        pltpu.VMEM((width, depth), BF16),
        pltpu.VMEM((nz, block, depth), BF16),
        pltpu.VMEM((nz, block, depth), BF16),
        pltpu.VMEM((depth, crops), BF16),
        pltpu.VMEM((depth, crops), BF16),
        pltpu.VMEM((crops, width), F32),
        pltpu.VMEM((crops, width), BF16),
        pltpu.VMEM((crops, width), BF16),
        pltpu.VMEM((8, width), F32),
        pltpu.VMEM((crops, LANES), F32),
        pltpu.VMEM((ITERS, 2, 1, width // 2), F32),
        pltpu.VMEM((groups, LANES), F32),
        pltpu.VMEM((groups, LANES), F32),
        pltpu.VMEM((ITERS, 2, groups // 2, LANES), BF16),
        pltpu.VMEM((groups, LANES), BF16),
        pltpu.VMEM((groups, LANES), F32),
        pltpu.VMEM((groups, LANES), F32),
        pltpu.VMEM((2, LANES, LANES), F32),
        pltpu.VMEM((ITERS, 2, b1, 1, width // 2), F32),
        pltpu.VMEM((ITERS, 2, nx * nz - 1, groups // 2, LANES), BF16),
        pltpu.VMEM((nx * nz - 1, groups, LANES), BF16),
        pltpu.VMEM((2, nz, block, depth), BF16),
        pltpu.VMEM((2, block, depth), F32),
        pltpu.VMEM((2, 2, block, depth), BF16),
        pltpu.VMEM((2, x1, nz, rows, depth), BF16),
        pltpu.VMEM((2, nz, rows, depth), BF16),
        pltpu.VMEM((2, nz, rows, depth), BF16),
        pltpu.VMEM((2, ny, dr, width), F32),
        pltpu.VMEM((2, ny, dr, width), BF16),
        pltpu.VMEM((ny, dr, width), BF16),
        pltpu.VMEM((y1, dr, width), BF16),
        pltpu.VMEM((y1, dr, width), BF16),
        dma((2,)),
        dma((nz,)), dma((nz,)), dma((2,)), dma((nz,)),
        dma((ITERS, 2)), dma((ITERS, 2)), dma, dma((2, 2)), dma((2, nz)), dma((2,)), dma((nch,)), dma((nch,)),
        dma, dma, dma, dma, dma((2,)), dma,
        pltpu.VMEM((nx * nz, rows, depth), BF16),
    ]
    outs = pl.pallas_call(
        functools.partial(kernel, nx, nz, ny),
        out_shape=(
            jax.ShapeDtypeStruct((dr, width), F32),
            jax.ShapeDtypeStruct((rows, depth), F32),
        ),
        in_specs=[vmem, vmem, hbm, hbm],
        out_specs=(vmem, vmem),
        scratch_shapes=scratch,
        compiler_params=pltpu.CompilerParams(
            collective_id=0, has_side_effects=True, vmem_limit_bytes=60 * 1024 * 1024
        ),
        cost_estimate=pl.CostEstimate(
            flops=12 * crops * width * depth, bytes_accessed=4 * depth * width,
            transcendentals=2 * crops * width,
        ),
    )(student_feats, teacher_feats, student_protos, teacher_protos)
    return pl.pallas_call(
        scale_out,
        out_shape=tuple(jax.ShapeDtypeStruct(o.shape, o.dtype) for o in outs),
        in_specs=[vmem, vmem],
        out_specs=(vmem, vmem),
    )(*outs)


def solution(mesh, nz=8):
    nx, ny = mesh.shape["proto"] // nz, mesh.shape["batch"] // 2
    in_specs = (
        P(("batch", "proto"), None),
        P(("batch", "proto"), None),
        P(None, "proto"),
        P(None, "proto"),
    )
    out_specs = (P("batch", "proto"), P(("batch", "proto"), None))
    return jax.shard_map(
        functools.partial(shards, nx, nz, ny),
        mesh=mesh, in_specs=in_specs, out_specs=out_specs, check_vma=False,
    )
```

```python
import functools

import jax
import jax.numpy as jnp
from jax import lax
from jax.experimental import pallas as pl
from jax.experimental.pallas import tpu as pltpu
from jax.sharding import PartitionSpec as P

ITERS = 3
STUDENT_TEMP = 0.1
TEACHER_TEMP = 0.07
LOG2E = 1.4426950408889634
MESH = pl.DeviceIdType.MESH
F32 = jnp.float32
BF16 = jnp.bfloat16
LANES = 128


def unit_rows(feats):
    values = feats.astype(F32)
    norm = jnp.sqrt(jnp.sum(values * values, axis=1, keepdims=True) + 1e-06)
    return values / norm, norm


def kernel(
    nx, nz, ny,
    sf, tf, sp_hbm, tp_hbm,
    pg_out, fg_out,
    tp, sp, spt, tall, uall, ut, uts, m, e, g,
    colacc, racc, ps, lse_acc, crop_acc, pay, pay_l, cinv, ccs, own_col,
    cb, pb, pbl,
    ugb, ug0, near, xr, zs, zr,
    pgf, pgb, cr, ys, yr,
    local_s,
    tz_r, tx_r, uz_r, ux_r, cb_r, pb_r, pbl_r, fn_r, fx_r, fz_r, pc_r, py_r,
    t_s, u_s, cb_s, pb_s, f_s, p_s,
    spare,
):
    rows = sf.shape[0]
    depth, width = tp.shape
    block = nx * rows
    crops = nz * block
    nb = 2 * ny
    dr = depth // nb
    tile = min(256, width)
    groups = crops // LANES
    per = block // LANES
    chunk = min(512, width)

    pid = lax.axis_index("proto")
    bid = lax.axis_index("batch")
    x, z = pid // nz, pid % nz
    y, c = bid // 2, bid % 2
    my = pl.multiple_of(x * rows, rows)

    def to_xz(xx, zz):
        return {"proto": (xx % nx) * nz + zz % nz}

    def to_b(bb):
        return {"batch": bb % nb}

    def remote(src, dst, ss, rs, dev):
        return pltpu.make_async_remote_copy(
            src_ref=src, dst_ref=dst, send_sem=ss, recv_sem=rs, device_id=dev, device_id_type=MESH
        )

    drain = []

    row_bytes = rows * depth * 2

    def landed(sem, count):
        if count:
            ref = spare.at[pl.ds(0, count)]
            remote(ref, ref, sem, sem, to_xz(x, z + 1)).wait_recv()

    def gone(sem, count):
        if count:
            ref = spare.at[pl.ds(0, count)]
            remote(ref, ref, sem, sem, to_xz(x, z + 1)).wait_send()

    barrier = pltpu.get_barrier_semaphore()
    for k in range(1, nx):
        pl.semaphore_signal(barrier, inc=1, device_id=to_xz(x + k, z), device_id_type=MESH)
    for k in range(1, nz):
        pl.semaphore_signal(barrier, inc=1, device_id=to_xz(x, z + k), device_id_type=MESH)
    for k in range(1, nb):
        pl.semaphore_signal(barrier, inc=1, device_id=to_b(bid + k), device_id_type=MESH)

    load_tp = pltpu.make_async_copy(tp_hbm, tp, local_s.at[0])
    load_sp = pltpu.make_async_copy(sp_hbm, sp, local_s.at[1])
    load_tp.start()
    load_sp.start()

    tall[z, pl.ds(my, rows), :] = unit_rows(tf[...])[0].astype(BF16)
    uall[z, pl.ds(my, rows), :] = unit_rows(sf[...])[0].astype(BF16)
    colacc[...] = jnp.zeros_like(colacc)
    eye = lax.broadcasted_iota(jnp.int32, (LANES, LANES), 0) == lax.broadcasted_iota(
        jnp.int32, (LANES, LANES), 1
    )

    def to_row(col):
        return jnp.sum(jnp.where(eye, col, 0.0), axis=0, keepdims=True)

    def to_col(row):
        return jnp.sum(jnp.where(eye, row, 0.0), axis=1, keepdims=True)

    pl.semaphore_wait(barrier, (nx - 1) + (nz - 1) + (nb - 1))

    near_z = sorted({1, nz - 1})
    far_z = [d for d in range(1, nz) if d not in near_z]
    far_z = sorted(far_z, key=lambda d: (min(d, nz - d), d))

    u_order = [d for d in range(1, nz)]
    cut = (len(u_order) - 1) // 2
    u_first, u_second = u_order[:cut], u_order[cut:]

    def tz(d):
        ref = tall.at[z, pl.ds(my, rows)]
        return remote(ref, ref, t_s, tz_r.at[d], to_xz(x, z + d))

    def trow(d):
        ref = tall.at[z]
        return remote(ref, ref, t_s, tz_r.at[d], to_xz(x, z + d))

    def tx(d, k):
        ref = tall.at[(z + nz - d) % nz, pl.ds(my, rows)]
        return remote(ref, ref, t_s, tx_r.at[d], to_xz(x + k, z))

    def uz(d):
        ref = uall.at[z, pl.ds(my, rows)]
        return remote(ref, ref, u_s, uz_r.at[0 if d in u_first else 1], to_xz(x, z + d))

    def ux(d, k):
        ref = uall.at[(z + nz - d) % nz, pl.ds(my, rows)]
        return remote(ref, ref, u_s, ux_r.at[d], to_xz(x + k, z))

    for k in range(1, nx):
        tx(0, k).start()
    for d in far_z:
        tz(d).start()

    def compute_m(blk):
        row0 = pl.multiple_of(blk * block, block)
        a = tall[blk]
        for j in range(width // tile):
            cols = slice(j * tile, (j + 1) * tile)
            s = jnp.dot(a, tp[:, cols], preferred_element_type=F32)
            v = jnp.exp2(s * (LOG2E / TEACHER_TEMP))
            m[pl.ds(row0, block), cols] = v
            colacc[:, cols] += jnp.sum(v.reshape(block // 8, 8, tile), axis=0)

    landed(tx_r.at[0], nx - 1)
    for d in near_z:
        trow(d).start()
    load_tp.wait()
    compute_m(z)
    for d in far_z:
        tz(d).wait_recv()
        for k in range(1, nx):
            tx(d, k).start()
    for k in range(1, nx):
        ux(0, k).start()
    for d in range(1, nz):
        uz(d).start()

    def pick(s, table):
        out = jnp.int32(table[0])
        for i in range(1, len(table)):
            out = jnp.where(s == i, table[i], out)
        return out

    arrivals = far_z[:2] + near_z + far_z[2:]

    @pl.loop(0, nz - 1)
    def _(s):
        d = pick(s, arrivals)
        is_near = (d == 1) | (d == nz - 1)

        @pl.when(is_near)
        def _():
            trow(d).wait_recv()

        @pl.when(jnp.logical_not(is_near))
        def _():
            landed(tx_r.at[d], nx - 1)

        compute_m((z + nz - d) % nz)

    drain.append(lambda: gone(t_s, (nx - 1) * (1 + len(far_z)) + len(far_z) + nx * len(near_z)))

    def cb_copy(it, h, k):
        return remote(
            ps.at[it, h], cb.at[it, h, k - 1], cb_s, cb_r.at[it, h], to_b(bid + k)
        )

    def pb_copy(it, h, kx, kz):
        i = kx * nz + kz - 1
        return remote(
            pay.at[it, h], pb.at[it, h, i], pb_s, pb_r.at[it, h], to_xz(x + kx, z + kz)
        )

    def pbl_copy(kx, kz):
        i = kx * nz + kz - 1
        return remote(pay_l, pbl.at[i], pb_s, pbl_r, to_xz(x + kx, z + kz))

    others = [(kx, kz) for kx in range(nx) for kz in range(nz) if kx or kz]
    others.sort(key=lambda p: -min(p[0], nx - p[0]) - min(p[1], nz - p[1]))

    def pb_total(it, h):
        remote(pb.at[it, h], pb.at[it, h], pb_s, pb_r.at[it, h], to_xz(x, z + 1)).wait_recv()
        total = pay[it, h].astype(F32)
        for i in range(nx * nz - 1):
            total = total + pb[it, h, i].astype(F32)
        return total

    def pbl_total():
        remote(pbl, pbl, pb_s, pbl_r, to_xz(x, z + 1)).wait_recv()
        total = pay_l[...].astype(F32)
        for i in range(nx * nz - 1):
            total = total + pbl[i].astype(F32)
        return total

    def compute_e(blk):
        row0 = pl.multiple_of(blk * block, block)
        a = uall[blk]
        ut[:, pl.ds(row0, block)] = a.T
        acc = jnp.zeros((block, LANES), F32)
        grad = jnp.zeros((block, depth), F32)
        for j in range(width // tile):
            cols = slice(j * tile, (j + 1) * tile)
            s = jnp.dot(a, sp[:, cols], preferred_element_type=F32)
            v = jnp.exp2(jnp.minimum(s * (LOG2E / STUDENT_TEMP), 128.0) - 18.0)
            half = v.astype(BF16)
            e[pl.ds(row0, block), cols] = half
            for t in range(tile // LANES):
                acc += v[:, t * LANES : (t + 1) * LANES]
            grad += jnp.dot(half, spt[cols, :], preferred_element_type=F32)
        ugb[0, blk] = grad.astype(BF16)
        for i in range(per):
            col = jnp.sum(acc[i * LANES : (i + 1) * LANES], axis=1, keepdims=True)
            lse_acc[pl.ds(blk * per + i, 1), :] = to_row(col)
        return grad

    def e_blocks(ds):
        @pl.loop(0, len(ds))
        def _(s):
            d = pick(s, ds)
            landed(ux_r.at[d], nx - 1)
            compute_e((z + nz - d) % nz)

    def u_forward(ds, i):
        landed(uz_r.at[i], len(ds))
        for d in ds:
            for k in range(1, nx):
                ux(d, k).start()

    hw, hg = width // 2, groups // 2

    def crop_col(i, keep):
        at = pl.ds(pl.multiple_of(i * LANES, LANES), LANES)
        if keep is None:
            return racc[at, :]
        col = jnp.broadcast_to(to_col(ccs[pl.ds(i, 1), :]), (LANES, LANES))
        if keep:
            racc[at, :] = col
        return col

    def colsum(h, lo, n, keep):
        def body(j, acc):
            i = h * hg + j
            col = crop_col(i, keep)
            for q in range(LANES // 8):
                at = pl.ds(pl.multiple_of(i * LANES + q * 8, 8), 8)
                w = col[q * 8 : (q + 1) * 8]
                acc = tuple(
                    a + m[at, lo + t * LANES : lo + (t + 1) * LANES] * w for t, a in enumerate(acc)
                )
            return acc

        init = tuple(jnp.zeros((8, LANES), F32) for _ in range(n // LANES))
        return jnp.concatenate(lax.fori_loop(0, hg, body, init, unroll=min(4, hg)), axis=1)

    def rowsum_first(scale):
        def body(i):
            at = pl.ds(pl.multiple_of(i * LANES, LANES), LANES)
            acc = jnp.zeros((LANES, LANES), F32)
            for t in range(hw // LANES):
                cols = slice(t * LANES, (t + 1) * LANES)
                acc = acc + m[at, cols] * scale[:, cols]
            racc[at, :] = acc

        pl.loop(0, groups, unroll=min(2, groups))(body)

    def rowsum_second(scale, h):
        def body(j):
            i = h * hg + j
            at = pl.ds(pl.multiple_of(i * LANES, LANES), LANES)
            acc = racc[at, :]
            for t in range(hw // LANES):
                cols = slice(t * LANES, (t + 1) * LANES)
                acc = acc + m[at, hw + t * LANES : hw + (t + 1) * LANES] * scale[:, cols]
            crop_acc[pl.ds(i, 1), :] = to_row(jnp.sum(acc, axis=1, keepdims=True))

        pl.loop(0, hg, unroll=min(4, hg))(body)

    late = far_z[::-1]
    nch = width // chunk

    def fn_copy(q, d):
        i = near_z.index(d)
        return remote(
            ugb.at[q, (z + d) % nz], near.at[q, i], f_s.at[q], fn_r.at[q, i], to_xz(x, z + d)
        )

    def fx_copy(q, d, k):
        xx = (x + k) % nx
        return remote(
            ugb.at[q, (z + d) % nz, pl.ds(pl.multiple_of(xx * rows, rows), rows)],
            xr.at[q, k - 1, d], f_s.at[q], fx_r.at[q, d], to_xz(xx, z),
        )

    def fz_copy(q, d):
        return remote(zs.at[q, d], zr.at[q, d], f_s.at[q], fz_r.at[q], to_xz(x, z + d))

    def x_sum(q, d):
        landed(fx_r.at[q, d], nx - 1)
        total = ugb[q, (z + d) % nz, pl.ds(my, rows), :].astype(F32) if d else ug0[q, pl.ds(my, rows), :]
        for k in range(1, nx):
            total = total + xr[q, k - 1, d].astype(F32)
        return total

    def z_send(q, d):
        zs[q, d] = x_sum(q, d).astype(BF16)
        fz_copy(q, d).start()

    def own_rows(q):
        total = ug0[q]
        for i, d in enumerate(near_z):
            fn_copy(q, d).wait_recv()
            total = total + near[q, i].astype(F32)
        ug0[q] = total
        ugb[q, z] = total.astype(BF16)
        for k in range(1, nx):
            fx_copy(q, 0, k).start()

    def f_send(q, d):
        if d in near_z:
            fn_copy(q, d).start()
        elif d:
            for k in range(1, nx):
                fx_copy(q, d, k).start()

    def f_total(q):
        total = x_sum(q, 0)
        landed(fz_r.at[q], len(late))
        for d in late:
            total = total + zr[q, d].astype(F32)
        return total

    series = near_z + late + [0]
    pairs = [series[i : i + 2] for i in range(0, nz, 2)]

    def targets(scale):
        @pl.loop(0, len(pairs))
        def _(s):
            blks = [(z + pick(s, [p[i] for p in pairs])) % nz for i in range(2)]
            scas = [
                jnp.concatenate([to_col(ccs[pl.ds(blk * per + i, 1), :]) for i in range(per)], axis=0)
                for blk in blks
            ]
            acc = jnp.zeros((2 * block, depth), F32)
            for j in range(width // tile):
                cols = slice(j * tile, (j + 1) * tile)
                both = []
                for blk, sca in zip(blks, scas):
                    at = pl.ds(pl.multiple_of(blk * block, block), block)
                    gh = ((m[at, cols] * sca) * scale[:, cols]).astype(BF16)
                    g[at, cols] = gh
                    both.append(gh)
                acc += jnp.dot(jnp.concatenate(both, axis=0), spt[cols, :], preferred_element_type=F32)
            for i, blk in enumerate(blks):
                ugb[1, blk] = acc[i * block : (i + 1) * block].astype(BF16)

            @pl.when(s == len(pairs) - 1)
            def _():
                ug0[1] = acc[block:]

            for i, p in enumerate(pairs):

                @pl.when(s == i)
                def _():
                    for d in p:
                        f_send(1, d)

    def scaled_ut(ref):
        def body(i):
            cols = pl.ds(pl.multiple_of(i * LANES, LANES), LANES)
            uts[:, cols] = (ut[:, cols].astype(F32) * ref[pl.ds(i, 1), :]).astype(BF16)

        pl.loop(0, groups, unroll=min(4, groups))(body)

    def probs_part():
        scaled_ut(cinv)

        @pl.loop(0, nch)
        def _(j):
            cols = pl.ds(pl.multiple_of(j * chunk, chunk), chunk)
            part = jnp.dot(uts[...], e[:, cols], preferred_element_type=F32)
            for yy in range(ny):
                for cc in range(2):
                    d0 = (yy * 2 + cc) * dr
                    pgf[cc, yy, :, cols] = part[d0 : d0 + dr]

    def send_ps(it, h, part):
        ps[it, h] = jnp.sum(part, axis=0, keepdims=True)
        for k in range(1, nb):
            cb_copy(it, h, k).start()

    def proto_scale(it, h):
        remote(cb.at[it, h], cb.at[it, h], cb_s, cb_r.at[it, h], to_b(bid + 1)).wait_recv()
        total = ps[it, h]
        for k in range(1, nb):
            total = total + cb[it, h, k - 1]
        return 1.0 / total

    def crop_half(h):
        return pl.ds(h * hg, hg)

    for it in range(ITERS):
        if it == 0:
            for h in range(2):
                send_ps(it, h, colacc[:, h * hw : (h + 1) * hw])
        else:
            ccs[crop_half(0), :] = 1.0 / pb_total(it - 1, 0)
            colacc[...] = colsum(0, 0, width, False)
            ccs[crop_half(1), :] = 1.0 / pb_total(it - 1, 1)
            for h in range(2):
                send_ps(it, h, colacc[:, h * hw : (h + 1) * hw] + colsum(1, h * hw, hw, None if h else True))
        if it == 0:
            load_sp.wait()

            @pl.loop(0, width // tile)
            def _(j):
                cols = pl.ds(pl.multiple_of(j * tile, tile), tile)
                spt[cols, :] = sp[:, cols].T

        elif it == 1:
            u_forward(u_second, 1)
            e_blocks(u_first)
        else:
            for d in u_second:
                f_send(0, nz - d)
        scales = [proto_scale(it, 0)]
        if it == 0:
            u_forward(u_first, 0)
        rowsum_first(scales[0])
        scales.append(proto_scale(it, 1))
        for h in range(2):
            rowsum_second(scales[1], h)
            pay[it, h] = crop_acc[crop_half(h), :].astype(BF16)
            for kx, kz in others:
                pb_copy(it, h, kx, kz).start()
        if it == 0:
            landed(ux_r.at[0], nx - 1)
            ug0[0] = compute_e(z)
        elif it == 1:
            for d in u_first:
                f_send(0, nz - d)
            e_blocks(u_second)
            pay_l[...] = lse_acc[...].astype(BF16)
            for kx, kz in others:
                pbl_copy(kx, kz).start()
        else:
            targets(jnp.concatenate(scales, axis=1))
            cinv[...] = 1.0 / pbl_total()
            own_rows(0)
            for d in late:
                z_send(0, d)
            probs_part()
    for h in range(2):
        ccs[crop_half(h), :] = 1.0 / (pb_total(ITERS - 1, h) * ccs[crop_half(h), :])

    drain.append(lambda: gone(u_s, (nx - 1) * nz + nz - 1))
    drain.append(lambda: remote(cb, cb, cb_s, cb_r.at[0, 0], to_b(bid + 1)).wait_send())
    drain.append(lambda: remote(pb, pb, pb_s, pb_r.at[0, 0], to_xz(x, z + 1)).wait_send())
    drain.append(lambda: remote(pbl, pbl, pb_s, pbl_r, to_xz(x, z + 1)).wait_send())

    def pc_copy(j):
        cols = pl.ds(pl.multiple_of(j * chunk, chunk), chunk)
        return remote(
            pgb.at[1 - c, :, :, cols], cr.at[:, :, cols], p_s, pc_r.at[j], to_b(y * 2 + 1 - c)
        )

    def py_copy(j, k):
        cols = pl.ds(pl.multiple_of(j * chunk, chunk), chunk)
        return remote(
            ys.at[k - 1, :, cols], yr.at[k - 1, :, cols],
            p_s, py_r.at[j], to_b(bid + 2 * k),
        )

    def pc_sum(j):
        cols = pl.ds(pl.multiple_of(j * chunk, chunk), chunk)
        pc_copy(j).wait_recv()
        for k in range(1, ny):
            yy = (y + k) % ny
            ys[k - 1, :, cols] = (pgf[c, yy, :, cols] + cr[yy, :, cols].astype(F32)).astype(BF16)
            py_copy(j, k).start()
        pg_out[:, cols] = pgf[c, y, :, cols] + cr[y, :, cols].astype(F32)

    scaled_ut(ccs)

    after = {0: ["own"] + late[:1], 1: late[1:2], 2: late[2:4]}
    after = {j: a for j, a in after.items() if j < nch}
    done = [d for a in after.values() for d in a]
    rest = (["own"] if "own" not in done else []) + [d for d in late if d not in done]

    def act(d):
        own_rows(1) if d == "own" else z_send(1, d)

    @pl.loop(0, nch)
    def _(j):
        cols = pl.ds(pl.multiple_of(j * chunk, chunk), chunk)
        part = jnp.dot(uts[...], g[:, cols], preferred_element_type=F32)
        for yy in range(ny):
            for cc in range(2):
                d0 = (yy * 2 + cc) * dr
                diff = pgf[cc, yy, :, cols] - part[d0 : d0 + dr]
                pgf[cc, yy, :, cols] = diff
                pgb[cc, yy, :, cols] = diff.astype(BF16)
        pc_copy(j).start()

        @pl.when(j > 0)
        def _():
            pc_sum(j - 1)

        for jj, ds in after.items():

            @pl.when(j == jj)
            def _():
                for d in ds:
                    act(d)

    pc_sum(nch - 1)
    for d in rest:
        act(d)
    part = z * per + my // LANES
    for q, ref in enumerate((cinv, ccs)):
        own_col[q] = jnp.broadcast_to(to_col(ref[pl.ds(part, 1), :]), (LANES, LANES))
    low = pl.multiple_of(my % LANES, min(rows, LANES))
    inv, rho = [own_col[q, pl.ds(low, rows), 0:1] for q in range(2)]
    total = f_total(0) * inv - f_total(1) * rho
    unit, norm = unit_rows(sf[...])
    inner = jnp.sum(unit * total, axis=1, keepdims=True)
    fg_out[...] = (total - unit * inner) / norm

    @pl.loop(0, nch)
    def _(j):
        cols = pl.ds(pl.multiple_of(j * chunk, chunk), chunk)
        total = pg_out[:, cols]
        landed(py_r.at[j], (ny - 1) * dr * chunk * 2 // row_bytes)
        for k in range(1, ny):
            total = total + yr[k - 1, :, cols].astype(F32)
        pg_out[:, cols] = total

    drain.append(lambda: gone(f_s.at[0], nx * len(near_z) + (nx - 1) * (len(late) + 1) + len(late)))
    drain.append(lambda: gone(f_s.at[1], nx * len(near_z) + (nx - 1) * (len(late) + 1) + len(late)))
    drain.append(lambda: gone(p_s, (2 * ny - 1) * dr * width * 2 // row_bytes))
    for leave in drain:
        leave()


def scale_out(a, b, a_out, b_out):
    a_out[...] = a[...] / STUDENT_TEMP
    b_out[...] = b[...] / STUDENT_TEMP


def shards(nx, nz, ny, student_feats, teacher_feats, student_protos, teacher_protos):
    rows, depth = student_feats.shape
    width = student_protos.shape[1]
    block, nb = nx * rows, 2 * ny
    crops, dr = nz * block, depth // nb
    groups = crops // LANES
    chunk = min(512, width)
    nch = width // chunk
    one = lambda n: max(n, 1)
    x1, y1, b1 = one(nx - 1), one(ny - 1), nb - 1
    dma = pltpu.SemaphoreType.DMA
    vmem = pl.BlockSpec(memory_space=pltpu.VMEM)
    hbm = pl.BlockSpec(memory_space=pl.ANY)
    scratch = [
        pltpu.VMEM((depth, width), BF16),
        pltpu.VMEM((depth, width), BF16),
        pltpu.VMEM((width, depth), BF16),
        pltpu.VMEM((nz, block, depth), BF16),
        pltpu.VMEM((nz, block, depth), BF16),
        pltpu.VMEM((depth, crops), BF16),
        pltpu.VMEM((depth, crops), BF16),
        pltpu.VMEM((crops, width), F32),
        pltpu.VMEM((crops, width), BF16),
        pltpu.VMEM((crops, width), BF16),
        pltpu.VMEM((8, width), F32),
        pltpu.VMEM((crops, LANES), F32),
        pltpu.VMEM((ITERS, 2, 1, width // 2), F32),
        pltpu.VMEM((groups, LANES), F32),
        pltpu.VMEM((groups, LANES), F32),
        pltpu.VMEM((ITERS, 2, groups // 2, LANES), BF16),
        pltpu.VMEM((groups, LANES), BF16),
        pltpu.VMEM((groups, LANES), F32),
        pltpu.VMEM((groups, LANES), F32),
        pltpu.VMEM((2, LANES, LANES), F32),
        pltpu.VMEM((ITERS, 2, b1, 1, width // 2), F32),
        pltpu.VMEM((ITERS, 2, nx * nz - 1, groups // 2, LANES), BF16),
        pltpu.VMEM((nx * nz - 1, groups, LANES), BF16),
        pltpu.VMEM((2, nz, block, depth), BF16),
        pltpu.VMEM((2, block, depth), F32),
        pltpu.VMEM((2, 2, block, depth), BF16),
        pltpu.VMEM((2, x1, nz, rows, depth), BF16),
        pltpu.VMEM((2, nz, rows, depth), BF16),
        pltpu.VMEM((2, nz, rows, depth), BF16),
        pltpu.VMEM((2, ny, dr, width), F32),
        pltpu.VMEM((2, ny, dr, width), BF16),
        pltpu.VMEM((ny, dr, width), BF16),
        pltpu.VMEM((y1, dr, width), BF16),
        pltpu.VMEM((y1, dr, width), BF16),
        dma((2,)),
        dma((nz,)), dma((nz,)), dma((2,)), dma((nz,)),
        dma((ITERS, 2)), dma((ITERS, 2)), dma, dma((2, 2)), dma((2, nz)), dma((2,)), dma((nch,)), dma((nch,)),
        dma, dma, dma, dma, dma((2,)), dma,
        pltpu.VMEM((nx * nz, rows, depth), BF16),
    ]
    outs = pl.pallas_call(
        functools.partial(kernel, nx, nz, ny),
        out_shape=(
            jax.ShapeDtypeStruct((dr, width), F32),
            jax.ShapeDtypeStruct((rows, depth), F32),
        ),
        in_specs=[vmem, vmem, hbm, hbm],
        out_specs=(vmem, vmem),
        scratch_shapes=scratch,
        compiler_params=pltpu.CompilerParams(
            collective_id=0, has_side_effects=True, vmem_limit_bytes=60 * 1024 * 1024
        ),
        cost_estimate=pl.CostEstimate(
            flops=12 * crops * width * depth, bytes_accessed=4 * depth * width,
            transcendentals=2 * crops * width,
        ),
    )(student_feats, teacher_feats, student_protos, teacher_protos)
    return pl.pallas_call(
        scale_out,
        out_shape=tuple(jax.ShapeDtypeStruct(o.shape, o.dtype) for o in outs),
        in_specs=[vmem, vmem],
        out_specs=(vmem, vmem),
    )(*outs)


def solution(mesh, nz=8):
    nx, ny = mesh.shape["proto"] // nz, mesh.shape["batch"] // 2
    in_specs = (
        P(("batch", "proto"), None),
        P(("batch", "proto"), None),
        P(None, "proto"),
        P(None, "proto"),
    )
    out_specs = (P("batch", "proto"), P(("batch", "proto"), None))
    return jax.shard_map(
        functools.partial(shards, nx, nz, ny),
        mesh=mesh, in_specs=in_specs, out_specs=out_specs, check_vma=False,
    )
```

```python
import functools

import jax
import jax.numpy as jnp
from jax import lax
from jax.experimental import pallas as pl
from jax.experimental.pallas import tpu as pltpu
from jax.sharding import PartitionSpec as P

ITERS = 3
STUDENT_TEMP = 0.1
TEACHER_TEMP = 0.07
LOG2E = 1.4426950408889634
MESH = pl.DeviceIdType.MESH
F32 = jnp.float32
BF16 = jnp.bfloat16
LANES = 128


def unit_rows(feats):
    values = feats.astype(F32)
    norm = jnp.sqrt(jnp.sum(values * values, axis=1, keepdims=True) + 1e-06)
    return values / norm, norm


def kernel(
    nx, nz, ny,
    sf, tf, sp_hbm, tp_hbm,
    pg_out, fg_out,
    tp, sp, spt, tall, uall, ut, uts, m, e, g,
    colacc, racc, ps, lse_acc, crop_acc, pay, pay_l, cinv, ccs, own_col,
    cb, pb, pbl,
    ugb, ug0, near, xr, zs, zr,
    pgf, pgb, cr, ys, yr,
    local_s,
    tz_r, tx_r, uz_r, ux_r, cb_r, pb_r, pbl_r, fn_r, fx_r, fz_r, pc_r, py_r,
    t_s, u_s, cb_s, pb_s, f_s, p_s,
    spare,
):
    rows = sf.shape[0]
    depth, width = tp.shape
    block = nx * rows
    crops = nz * block
    nb = 2 * ny
    dr = depth // nb
    tile = min(256, width)
    groups = crops // LANES
    per = block // LANES
    chunk = min(512, width)

    pid = lax.axis_index("proto")
    bid = lax.axis_index("batch")
    x, z = pid // nz, pid % nz
    y, c = bid // 2, bid % 2
    my = pl.multiple_of(x * rows, rows)

    def to_xz(xx, zz):
        return {"proto": (xx % nx) * nz + zz % nz}

    def to_b(bb):
        return {"batch": bb % nb}

    def remote(src, dst, ss, rs, dev):
        return pltpu.make_async_remote_copy(
            src_ref=src, dst_ref=dst, send_sem=ss, recv_sem=rs, device_id=dev, device_id_type=MESH
        )

    drain = []

    row_bytes = rows * depth * 2

    def landed(sem, count):
        if count:
            ref = spare.at[pl.ds(0, count)]
            remote(ref, ref, sem, sem, to_xz(x, z + 1)).wait_recv()

    def gone(sem, count):
        if count:
            ref = spare.at[pl.ds(0, count)]
            remote(ref, ref, sem, sem, to_xz(x, z + 1)).wait_send()

    barrier = pltpu.get_barrier_semaphore()
    for k in range(1, nx):
        pl.semaphore_signal(barrier, inc=1, device_id=to_xz(x + k, z), device_id_type=MESH)
    for k in range(1, nz):
        pl.semaphore_signal(barrier, inc=1, device_id=to_xz(x, z + k), device_id_type=MESH)
    for k in range(1, nb):
        pl.semaphore_signal(barrier, inc=1, device_id=to_b(bid + k), device_id_type=MESH)

    load_tp = pltpu.make_async_copy(tp_hbm, tp, local_s.at[0])
    load_sp = pltpu.make_async_copy(sp_hbm, sp, local_s.at[1])
    load_tp.start()
    load_sp.start()

    tall[z, pl.ds(my, rows), :] = unit_rows(tf[...])[0].astype(BF16)
    uall[z, pl.ds(my, rows), :] = unit_rows(sf[...])[0].astype(BF16)
    colacc[...] = jnp.zeros_like(colacc)
    eye = lax.broadcasted_iota(jnp.int32, (LANES, LANES), 0) == lax.broadcasted_iota(
        jnp.int32, (LANES, LANES), 1
    )

    def to_row(col):
        return jnp.sum(jnp.where(eye, col, 0.0), axis=0, keepdims=True)

    def to_col(row):
        return jnp.sum(jnp.where(eye, row, 0.0), axis=1, keepdims=True)

    pl.semaphore_wait(barrier, (nx - 1) + (nz - 1) + (nb - 1))

    near_z = sorted({1, nz - 1})
    far_z = [d for d in range(1, nz) if d not in near_z]
    far_z = sorted(far_z, key=lambda d: (min(d, nz - d), d))

    u_order = [d for d in range(1, nz)]
    cut = (len(u_order) - 1) // 2
    u_first, u_second = u_order[:cut], u_order[cut:]

    def tz(d):
        ref = tall.at[z, pl.ds(my, rows)]
        return remote(ref, ref, t_s, tz_r.at[d], to_xz(x, z + d))

    def trow(d):
        ref = tall.at[z]
        return remote(ref, ref, t_s, tz_r.at[d], to_xz(x, z + d))

    def tx(d, k):
        ref = tall.at[(z + nz - d) % nz, pl.ds(my, rows)]
        return remote(ref, ref, t_s, tx_r.at[d], to_xz(x + k, z))

    def uz(d):
        ref = uall.at[z, pl.ds(my, rows)]
        return remote(ref, ref, u_s, uz_r.at[0 if d in u_first else 1], to_xz(x, z + d))

    def ux(d, k):
        ref = uall.at[(z + nz - d) % nz, pl.ds(my, rows)]
        return remote(ref, ref, u_s, ux_r.at[d], to_xz(x + k, z))

    for k in range(1, nx):
        tx(0, k).start()
    for d in far_z:
        tz(d).start()

    def compute_m(blk):
        row0 = pl.multiple_of(blk * block, block)
        a = tall[blk]
        for j in range(width // tile):
            cols = slice(j * tile, (j + 1) * tile)
            s = jnp.dot(a, tp[:, cols], preferred_element_type=F32)
            v = jnp.exp2(s * (LOG2E / TEACHER_TEMP))
            m[pl.ds(row0, block), cols] = v
            colacc[:, cols] += jnp.sum(v.reshape(block // 8, 8, tile), axis=0)

    landed(tx_r.at[0], nx - 1)
    for d in near_z:
        trow(d).start()
    load_tp.wait()
    for i, d in enumerate(far_z):
        if i == min(2, len(far_z) - 1):
            compute_m(z)
        tz(d).wait_recv()
        for k in range(1, nx):
            tx(d, k).start()
    for k in range(1, nx):
        ux(0, k).start()
    for d in range(1, nz):
        uz(d).start()

    def pick(s, table):
        out = jnp.int32(table[0])
        for i in range(1, len(table)):
            out = jnp.where(s == i, table[i], out)
        return out

    arrivals = far_z[:2] + near_z + far_z[2:]

    @pl.loop(0, nz - 1)
    def _(s):
        d = pick(s, arrivals)
        is_near = (d == 1) | (d == nz - 1)

        @pl.when(is_near)
        def _():
            trow(d).wait_recv()

        @pl.when(jnp.logical_not(is_near))
        def _():
            landed(tx_r.at[d], nx - 1)

        compute_m((z + nz - d) % nz)

    drain.append(lambda: gone(t_s, (nx - 1) * (1 + len(far_z)) + len(far_z) + nx * len(near_z)))

    def cb_copy(it, h, k):
        return remote(
            ps.at[it, h], cb.at[it, h, k - 1], cb_s, cb_r.at[it, h], to_b(bid + k)
        )

    def pb_copy(it, h, kx, kz):
        i = kx * nz + kz - 1
        return remote(
            pay.at[it, h], pb.at[it, h, i], pb_s, pb_r.at[it, h], to_xz(x + kx, z + kz)
        )

    def pbl_copy(kx, kz):
        i = kx * nz + kz - 1
        return remote(pay_l, pbl.at[i], pb_s, pbl_r, to_xz(x + kx, z + kz))

    others = [(kx, kz) for kx in range(nx) for kz in range(nz) if kx or kz]
    others.sort(key=lambda p: -min(p[0], nx - p[0]) - min(p[1], nz - p[1]))

    def pb_total(it, h):
        remote(pb.at[it, h], pb.at[it, h], pb_s, pb_r.at[it, h], to_xz(x, z + 1)).wait_recv()
        total = pay[it, h].astype(F32)
        for i in range(nx * nz - 1):
            total = total + pb[it, h, i].astype(F32)
        return total

    def pbl_total():
        remote(pbl, pbl, pb_s, pbl_r, to_xz(x, z + 1)).wait_recv()
        total = pay_l[...].astype(F32)
        for i in range(nx * nz - 1):
            total = total + pbl[i].astype(F32)
        return total

    def compute_e(blk):
        row0 = pl.multiple_of(blk * block, block)
        a = uall[blk]
        ut[:, pl.ds(row0, block)] = a.T
        acc = jnp.zeros((block, LANES), F32)
        grad = jnp.zeros((block, depth), F32)
        for j in range(width // tile):
            cols = slice(j * tile, (j + 1) * tile)
            s = jnp.dot(a, sp[:, cols], preferred_element_type=F32)
            v = jnp.exp2(jnp.minimum(s * (LOG2E / STUDENT_TEMP), 128.0) - 2.0)
            half = v.astype(BF16)
            e[pl.ds(row0, block), cols] = half
            for t in range(tile // LANES):
                acc += v[:, t * LANES : (t + 1) * LANES]
            grad += jnp.dot(half, spt[cols, :], preferred_element_type=F32)
        ugb[0, blk] = grad.astype(BF16)
        for i in range(per):
            col = jnp.sum(acc[i * LANES : (i + 1) * LANES], axis=1, keepdims=True)
            lse_acc[pl.ds(blk * per + i, 1), :] = to_row(col)
        return grad

    def e_blocks(ds):
        @pl.loop(0, len(ds))
        def _(s):
            d = pick(s, ds)
            landed(ux_r.at[d], nx - 1)
            compute_e((z + nz - d) % nz)

    def u_forward(ds, i):
        landed(uz_r.at[i], len(ds))
        for d in ds:
            for k in range(1, nx):
                ux(d, k).start()

    hw, hg = width // 2, groups // 2

    def crop_col(i, keep):
        at = pl.ds(pl.multiple_of(i * LANES, LANES), LANES)
        if keep is None:
            return racc[at, :]
        col = jnp.broadcast_to(to_col(ccs[pl.ds(i, 1), :]), (LANES, LANES))
        if keep:
            racc[at, :] = col
        return col

    def colsum(h, lo, n, keep):
        def body(j, acc):
            i = h * hg + j
            col = crop_col(i, keep)
            for q in range(LANES // 8):
                at = pl.ds(pl.multiple_of(i * LANES + q * 8, 8), 8)
                w = col[q * 8 : (q + 1) * 8]
                acc = tuple(
                    a + m[at, lo + t * LANES : lo + (t + 1) * LANES] * w for t, a in enumerate(acc)
                )
            return acc

        init = tuple(jnp.zeros((8, LANES), F32) for _ in range(n // LANES))
        return jnp.concatenate(lax.fori_loop(0, hg, body, init, unroll=min(4, hg)), axis=1)

    def rowsum_first(scale):
        def body(i):
            at = pl.ds(pl.multiple_of(i * LANES, LANES), LANES)
            acc = jnp.zeros((LANES, LANES), F32)
            for t in range(hw // LANES):
                cols = slice(t * LANES, (t + 1) * LANES)
                acc = acc + m[at, cols] * scale[:, cols]
            racc[at, :] = acc

        pl.loop(0, groups, unroll=min(2, groups))(body)

    def rowsum_second(scale, h):
        def body(j):
            i = h * hg + j
            at = pl.ds(pl.multiple_of(i * LANES, LANES), LANES)
            acc = racc[at, :]
            for t in range(hw // LANES):
                cols = slice(t * LANES, (t + 1) * LANES)
                acc = acc + m[at, hw + t * LANES : hw + (t + 1) * LANES] * scale[:, cols]
            crop_acc[pl.ds(i, 1), :] = to_row(jnp.sum(acc, axis=1, keepdims=True))

        pl.loop(0, hg, unroll=min(4, hg))(body)

    late = far_z[::-1]
    nch = width // chunk

    def fn_copy(q, d):
        i = near_z.index(d)
        return remote(
            ugb.at[q, (z + d) % nz], near.at[q, i], f_s.at[q], fn_r.at[q, i], to_xz(x, z + d)
        )

    def fx_copy(q, d, k):
        xx = (x + k) % nx
        return remote(
            ugb.at[q, (z + d) % nz, pl.ds(pl.multiple_of(xx * rows, rows), rows)],
            xr.at[q, k - 1, d], f_s.at[q], fx_r.at[q, d], to_xz(xx, z),
        )

    def fz_copy(q, d):
        return remote(zs.at[q, d], zr.at[q, d], f_s.at[q], fz_r.at[q], to_xz(x, z + d))

    def x_sum(q, d):
        landed(fx_r.at[q, d], nx - 1)
        total = ugb[q, (z + d) % nz, pl.ds(my, rows), :].astype(F32) if d else ug0[q, pl.ds(my, rows), :]
        for k in range(1, nx):
            total = total + xr[q, k - 1, d].astype(F32)
        return total

    def z_send(q, d):
        zs[q, d] = x_sum(q, d).astype(BF16)
        fz_copy(q, d).start()

    def own_rows(q):
        total = ug0[q]
        for i, d in enumerate(near_z):
            fn_copy(q, d).wait_recv()
            total = total + near[q, i].astype(F32)
        ug0[q] = total
        ugb[q, z] = total.astype(BF16)
        for k in range(1, nx):
            fx_copy(q, 0, k).start()

    def f_send(q, d):
        if d in near_z:
            fn_copy(q, d).start()
        elif d:
            for k in range(1, nx):
                fx_copy(q, d, k).start()

    def f_total(q):
        total = x_sum(q, 0)
        landed(fz_r.at[q], len(late))
        for d in late:
            total = total + zr[q, d].astype(F32)
        return total

    series = near_z + late + [0]
    pairs = [series[i : i + 2] for i in range(0, nz, 2)]

    def targets(scale):
        @pl.loop(0, len(pairs))
        def _(s):
            blks = [(z + pick(s, [p[i] for p in pairs])) % nz for i in range(2)]
            scas = [
                jnp.concatenate([to_col(ccs[pl.ds(blk * per + i, 1), :]) for i in range(per)], axis=0)
                for blk in blks
            ]
            acc = jnp.zeros((2 * block, depth), F32)
            for j in range(width // tile):
                cols = slice(j * tile, (j + 1) * tile)
                both = []
                for blk, sca in zip(blks, scas):
                    at = pl.ds(pl.multiple_of(blk * block, block), block)
                    gh = ((m[at, cols] * sca) * scale[:, cols]).astype(BF16)
                    g[at, cols] = gh
                    both.append(gh)
                acc += jnp.dot(jnp.concatenate(both, axis=0), spt[cols, :], preferred_element_type=F32)
            for i, blk in enumerate(blks):
                ugb[1, blk] = acc[i * block : (i + 1) * block].astype(BF16)

            @pl.when(s == len(pairs) - 1)
            def _():
                ug0[1] = acc[block:]

            for i, p in enumerate(pairs):

                @pl.when(s == i)
                def _():
                    for d in p:
                        f_send(1, d)

    def scaled_ut(ref, factor=1.0):
        def body(i):
            cols = pl.ds(pl.multiple_of(i * LANES, LANES), LANES)
            uts[:, cols] = (ut[:, cols].astype(F32) * (ref[pl.ds(i, 1), :] * factor)).astype(BF16)

        pl.loop(0, groups, unroll=min(4, groups))(body)

    def probs_part():
        scaled_ut(cinv, 4096.0)

        @pl.loop(0, nch)
        def _(j):
            cols = pl.ds(pl.multiple_of(j * chunk, chunk), chunk)
            part = jnp.dot(uts[...], e[:, cols], preferred_element_type=F32)
            for yy in range(ny):
                for cc in range(2):
                    d0 = (yy * 2 + cc) * dr
                    pgf[cc, yy, :, cols] = part[d0 : d0 + dr] * (1.0 / 4096.0)

    def send_ps(it, h, part):
        ps[it, h] = jnp.sum(part, axis=0, keepdims=True)
        for k in range(1, nb):
            cb_copy(it, h, k).start()

    def proto_scale(it, h):
        remote(cb.at[it, h], cb.at[it, h], cb_s, cb_r.at[it, h], to_b(bid + 1)).wait_recv()
        total = ps[it, h]
        for k in range(1, nb):
            total = total + cb[it, h, k - 1]
        return 1.0 / total

    def crop_half(h):
        return pl.ds(h * hg, hg)

    for it in range(ITERS):
        if it == 0:
            for h in range(2):
                send_ps(it, h, colacc[:, h * hw : (h + 1) * hw])
        else:
            ccs[crop_half(0), :] = 1.0 / pb_total(it - 1, 0)
            colacc[...] = colsum(0, 0, width, False)
            ccs[crop_half(1), :] = 1.0 / pb_total(it - 1, 1)
            for h in range(2):
                send_ps(it, h, colacc[:, h * hw : (h + 1) * hw] + colsum(1, h * hw, hw, None if h else True))
        if it == 0:
            load_sp.wait()

            @pl.loop(0, width // tile)
            def _(j):
                cols = pl.ds(pl.multiple_of(j * tile, tile), tile)
                spt[cols, :] = sp[:, cols].T

        elif it == 1:
            u_forward(u_second, 1)
            e_blocks(u_first)
        else:
            for d in u_second:
                f_send(0, nz - d)
        scales = [proto_scale(it, 0)]
        if it == 0:
            u_forward(u_first, 0)
        rowsum_first(scales[0])
        scales.append(proto_scale(it, 1))
        for h in range(2):
            rowsum_second(scales[1], h)
            pay[it, h] = crop_acc[crop_half(h), :].astype(BF16)
            for kx, kz in others:
                pb_copy(it, h, kx, kz).start()
        if it == 0:
            landed(ux_r.at[0], nx - 1)
            ug0[0] = compute_e(z)
        elif it == 1:
            for d in u_first:
                f_send(0, nz - d)
            e_blocks(u_second)
            pay_l[...] = lse_acc[...].astype(BF16)
            for kx, kz in others:
                pbl_copy(kx, kz).start()
        else:
            targets(jnp.concatenate(scales, axis=1))
            cinv[...] = 1.0 / pbl_total()
            own_rows(0)
            for d in late:
                z_send(0, d)
            probs_part()
    for h in range(2):
        ccs[crop_half(h), :] = 1.0 / (pb_total(ITERS - 1, h) * ccs[crop_half(h), :])

    drain.append(lambda: gone(u_s, (nx - 1) * nz + nz - 1))
    drain.append(lambda: remote(cb, cb, cb_s, cb_r.at[0, 0], to_b(bid + 1)).wait_send())
    drain.append(lambda: remote(pb, pb, pb_s, pb_r.at[0, 0], to_xz(x, z + 1)).wait_send())
    drain.append(lambda: remote(pbl, pbl, pb_s, pbl_r, to_xz(x, z + 1)).wait_send())

    def pc_copy(j):
        cols = pl.ds(pl.multiple_of(j * chunk, chunk), chunk)
        return remote(
            pgb.at[1 - c, :, :, cols], cr.at[:, :, cols], p_s, pc_r.at[j], to_b(y * 2 + 1 - c)
        )

    def py_copy(j, k):
        cols = pl.ds(pl.multiple_of(j * chunk, chunk), chunk)
        return remote(
            ys.at[k - 1, :, cols], yr.at[k - 1, :, cols],
            p_s, py_r.at[j], to_b(bid + 2 * k),
        )

    def pc_sum(j):
        cols = pl.ds(pl.multiple_of(j * chunk, chunk), chunk)
        pc_copy(j).wait_recv()
        for k in range(1, ny):
            yy = (y + k) % ny
            ys[k - 1, :, cols] = (pgf[c, yy, :, cols] + cr[yy, :, cols].astype(F32)).astype(BF16)
            py_copy(j, k).start()
        pg_out[:, cols] = pgf[c, y, :, cols] + cr[y, :, cols].astype(F32)

    scaled_ut(ccs)

    after = {0: ["own"] + late[:1], 1: late[1:2], 2: late[2:4]}
    after = {j: a for j, a in after.items() if j < nch}
    done = [d for a in after.values() for d in a]
    rest = (["own"] if "own" not in done else []) + [d for d in late if d not in done]

    def act(d):
        own_rows(1) if d == "own" else z_send(1, d)

    @pl.loop(0, nch)
    def _(j):
        cols = pl.ds(pl.multiple_of(j * chunk, chunk), chunk)
        part = jnp.dot(uts[...], g[:, cols], preferred_element_type=F32)
        for yy in range(ny):
            for cc in range(2):
                d0 = (yy * 2 + cc) * dr
                diff = pgf[cc, yy, :, cols] - part[d0 : d0 + dr]
                pgf[cc, yy, :, cols] = diff
                pgb[cc, yy, :, cols] = diff.astype(BF16)
        pc_copy(j).start()

        @pl.when(j > 0)
        def _():
            pc_sum(j - 1)

        for jj, ds in after.items():

            @pl.when(j == jj)
            def _():
                for d in ds:
                    act(d)

    pc_sum(nch - 1)
    for d in rest:
        act(d)
    part = z * per + my // LANES
    for q, ref in enumerate((cinv, ccs)):
        own_col[q] = jnp.broadcast_to(to_col(ref[pl.ds(part, 1), :]), (LANES, LANES))
    low = pl.multiple_of(my % LANES, min(rows, LANES))
    inv, rho = [own_col[q, pl.ds(low, rows), 0:1] for q in range(2)]
    total = jnp.where(inv > 0.0, f_total(0) * inv, 0.0) - f_total(1) * rho
    unit, norm = unit_rows(sf[...])
    inner = jnp.sum(unit * total, axis=1, keepdims=True)
    fg_out[...] = (total - unit * inner) / norm

    @pl.loop(0, nch)
    def _(j):
        cols = pl.ds(pl.multiple_of(j * chunk, chunk), chunk)
        total = pg_out[:, cols]
        landed(py_r.at[j], (ny - 1) * dr * chunk * 2 // row_bytes)
        for k in range(1, ny):
            total = total + yr[k - 1, :, cols].astype(F32)
        pg_out[:, cols] = total

    drain.append(lambda: gone(f_s.at[0], nx * len(near_z) + (nx - 1) * (len(late) + 1) + len(late)))
    drain.append(lambda: gone(f_s.at[1], nx * len(near_z) + (nx - 1) * (len(late) + 1) + len(late)))
    drain.append(lambda: gone(p_s, (2 * ny - 1) * dr * width * 2 // row_bytes))
    for leave in drain:
        leave()


def scale_out(a, b, a_out, b_out):
    a_out[...] = a[...] / STUDENT_TEMP
    b_out[...] = b[...] / STUDENT_TEMP


def shards(nx, nz, ny, student_feats, teacher_feats, student_protos, teacher_protos):
    rows, depth = student_feats.shape
    width = student_protos.shape[1]
    block, nb = nx * rows, 2 * ny
    crops, dr = nz * block, depth // nb
    groups = crops // LANES
    chunk = min(512, width)
    nch = width // chunk
    one = lambda n: max(n, 1)
    x1, y1, b1 = one(nx - 1), one(ny - 1), nb - 1
    dma = pltpu.SemaphoreType.DMA
    vmem = pl.BlockSpec(memory_space=pltpu.VMEM)
    hbm = pl.BlockSpec(memory_space=pl.ANY)
    scratch = [
        pltpu.VMEM((depth, width), BF16),
        pltpu.VMEM((depth, width), BF16),
        pltpu.VMEM((width, depth), BF16),
        pltpu.VMEM((nz, block, depth), BF16),
        pltpu.VMEM((nz, block, depth), BF16),
        pltpu.VMEM((depth, crops), BF16),
        pltpu.VMEM((depth, crops), BF16),
        pltpu.VMEM((crops, width), F32),
        pltpu.VMEM((crops, width), BF16),
        pltpu.VMEM((crops, width), BF16),
        pltpu.VMEM((8, width), F32),
        pltpu.VMEM((crops, LANES), F32),
        pltpu.VMEM((ITERS, 2, 1, width // 2), F32),
        pltpu.VMEM((groups, LANES), F32),
        pltpu.VMEM((groups, LANES), F32),
        pltpu.VMEM((ITERS, 2, groups // 2, LANES), BF16),
        pltpu.VMEM((groups, LANES), BF16),
        pltpu.VMEM((groups, LANES), F32),
        pltpu.VMEM((groups, LANES), F32),
        pltpu.VMEM((2, LANES, LANES), F32),
        pltpu.VMEM((ITERS, 2, b1, 1, width // 2), F32),
        pltpu.VMEM((ITERS, 2, nx * nz - 1, groups // 2, LANES), BF16),
        pltpu.VMEM((nx * nz - 1, groups, LANES), BF16),
        pltpu.VMEM((2, nz, block, depth), BF16),
        pltpu.VMEM((2, block, depth), F32),
        pltpu.VMEM((2, 2, block, depth), BF16),
        pltpu.VMEM((2, x1, nz, rows, depth), BF16),
        pltpu.VMEM((2, nz, rows, depth), BF16),
        pltpu.VMEM((2, nz, rows, depth), BF16),
        pltpu.VMEM((2, ny, dr, width), F32),
        pltpu.VMEM((2, ny, dr, width), BF16),
        pltpu.VMEM((ny, dr, width), BF16),
        pltpu.VMEM((y1, dr, width), BF16),
        pltpu.VMEM((y1, dr, width), BF16),
        dma((2,)),
        dma((nz,)), dma((nz,)), dma((2,)), dma((nz,)),
        dma((ITERS, 2)), dma((ITERS, 2)), dma, dma((2, 2)), dma((2, nz)), dma((2,)), dma((nch,)), dma((nch,)),
        dma, dma, dma, dma, dma((2,)), dma,
        pltpu.VMEM((nx * nz, rows, depth), BF16),
    ]
    outs = pl.pallas_call(
        functools.partial(kernel, nx, nz, ny),
        out_shape=(
            jax.ShapeDtypeStruct((dr, width), F32),
            jax.ShapeDtypeStruct((rows, depth), F32),
        ),
        in_specs=[vmem, vmem, hbm, hbm],
        out_specs=(vmem, vmem),
        scratch_shapes=scratch,
        compiler_params=pltpu.CompilerParams(
            collective_id=0, has_side_effects=True, vmem_limit_bytes=60 * 1024 * 1024
        ),
        cost_estimate=pl.CostEstimate(
            flops=12 * crops * width * depth, bytes_accessed=4 * depth * width,
            transcendentals=2 * crops * width,
        ),
    )(student_feats, teacher_feats, student_protos, teacher_protos)
    return pl.pallas_call(
        scale_out,
        out_shape=tuple(jax.ShapeDtypeStruct(o.shape, o.dtype) for o in outs),
        in_specs=[vmem, vmem],
        out_specs=(vmem, vmem),
    )(*outs)


def solution(mesh, nz=8):
    nx, ny = mesh.shape["proto"] // nz, mesh.shape["batch"] // 2
    in_specs = (
        P(("batch", "proto"), None),
        P(("batch", "proto"), None),
        P(None, "proto"),
        P(None, "proto"),
    )
    out_specs = (P("batch", "proto"), P(("batch", "proto"), None))
    return jax.shard_map(
        functools.partial(shards, nx, nz, ny),
        mesh=mesh, in_specs=in_specs, out_specs=out_specs, check_vma=False,
    )
```
